256 devices in a mesh: lon: 32 (over z_lo, x, core), lat: 8 (over y, z_hi).
Axes of the slice: x: 4, y: 4, z: 8 (z_hi: 2, z_lo: 4; z = z_hi * 4 + z_lo), core: 2. Of those that a mesh axis runs over, the one named last changes fastest.
Arguments:
- tracers: float32 [6, 128, 64, 4096], P(None, None, 'lat', 'lon'), may hold values from 0.2 to 5
- courant_x: float32 [128, 64, 4096], P(None, 'lat', 'lon'), may hold values from -0.24 to 0.24
- courant_y: float32 [128, 64, 4096], P(None, 'lat', 'lon'), may hold values from -0.24 to 0.24
- sunlit: int32 [64, 4096], P('lat', 'lon'), may hold values from 0 to 1, as said below
- cosine_zenith: float32 [64, 4096], P('lat', 'lon'), may hold values from 0.1 to 1
- albedo: float32 [64, 4096], P('lat', 'lon'), may hold values from 0.05 to 0.7
- absorb: float32 [8, 6], replicated, may hold values from 0.0002 to 0.01
- scatter: float32 [8], replicated, may hold values from 0.001 to 0.05
- solar_weight: float32 [8], replicated, may hold values from 0.2 to 2
Outputs:
- tracers_next: float32 [6, 128, 64, 4096], P(None, None, 'lat', 'lon')
- heating: float32 [128, 64, 4096], P(None, 'lat', 'lon')
The draws below stay inside these ranges and needn't reach their ends.
Inputs may be any that keep to these rules, and one draw needn't show every extreme that they name: Of two columns in one latitude row 2048 longitudes apart, exactly one is sunlit; in each row the sunlit columns form one run of 2048 longitudes around the cycle.
All inputs are finite; a program needn't handle non-finite values.
Results may differ from the reference program's by a relative error of at most 0.00005.
Values sent between devices are 32-bit elements; how exact they have to be, the bound alone decides.
A program may use at most 128 MiB of HBM per device.

```python
import math
import jax
import jax.numpy as jnp
from jax import lax

LEVELS = 128
TRACERS = 6
GPOINTS = 8
LONS = 4096
LATS = 64


def draw_sunlit(key, part):
    key = jax.random.fold_in(key, 11)
    key_noon, key_shift = jax.random.split(key)
    noon_index = jax.random.randint(key_noon, (), 0, LONS)
    row_shift = jax.random.randint(key_shift, (LATS,), -(LONS // 16), LONS // 16 + 1)
    longitude = jnp.arange(LONS, dtype=jnp.int32)[None, :]
    offset = (longitude - noon_index - row_shift[:, None]) % LONS
    return (offset < LONS // 2).astype(jnp.int32)


def levels(stream_key, extent, shards, smallest, largest):
    def one(position, blocks):
        steps = jax.random.uniform(jax.random.fold_in(jax.random.fold_in(stream_key, 6), position), (blocks,), jnp.float32, smallest / len(shards), largest / len(shards))
        return jnp.repeat(jnp.exp(steps), extent[position] // blocks).reshape((-1,) + (1,) * (len(extent) - position - 1))

    gain = one(*shards[0])
    for cut in shards[1:]:
        gain = gain * one(*cut)
    return gain


def setup_inputs(seed: int = 0) -> dict:
    arg_keys = jax.random.split(jax.random.key(seed), 10)
    return {
        "tracers": jnp.clip(jnp.exp(math.log(5.0) - 3.218876 * jax.random.uniform(arg_keys[0], (TRACERS, LEVELS, LATS, LONS), jnp.float32) ** levels(arg_keys[0], (TRACERS, LEVELS, LATS, LONS), ((2, 8), (3, 32)), -0.2, 0.2)), 0.2, 5.0),
        "courant_x": jnp.clip(jax.random.uniform(arg_keys[1], (LEVELS, LATS, LONS), jnp.float32, -0.24, 0.24) * levels(arg_keys[1], (LEVELS, LATS, LONS), ((1, 8), (2, 32)), -0.4, 0.0), -0.24, 0.24),
        "courant_y": jnp.clip(jax.random.uniform(arg_keys[2], (LEVELS, LATS, LONS), jnp.float32, -0.24, 0.24) * levels(arg_keys[2], (LEVELS, LATS, LONS), ((1, 8), (2, 32)), -0.4, 0.0), -0.24, 0.24),
        "sunlit": draw_sunlit(jax.random.fold_in(arg_keys[9], 71), 0),
        "cosine_zenith": jnp.clip(0.1 + 0.9 * jax.random.uniform(arg_keys[4], (LATS, LONS), jnp.float32) ** levels(arg_keys[4], (LATS, LONS), ((0, 8), (1, 32)), -0.2, 0.2), 0.1, 1.0),
        "albedo": jnp.clip(0.05 + 0.65 * jax.random.uniform(arg_keys[5], (LATS, LONS), jnp.float32) ** levels(arg_keys[5], (LATS, LONS), ((0, 8), (1, 32)), -0.2, 0.2), 0.05, 0.7),
        "absorb": jnp.clip(jnp.exp(jax.random.uniform(arg_keys[6], (GPOINTS, TRACERS), jnp.float32, math.log(0.0002), math.log(0.01))), 0.0002, 0.01),
        "scatter": jnp.clip(jnp.exp(jax.random.uniform(arg_keys[7], (GPOINTS,), jnp.float32, math.log(0.001), math.log(0.05))), 0.001, 0.05),
        "solar_weight": jnp.clip(jnp.exp(jax.random.uniform(arg_keys[8], (GPOINTS,), jnp.float32, math.log(0.2), math.log(2.0))), 0.2, 2.0),
    }


asymmetry = 0.85
backscatter = 0.075
single_cap = 0.9
heat_scale = 4.0

def upwind(courant, current, forward):
    return jnp.maximum(courant, 0.0) * current + jnp.minimum(courant, 0.0) * forward

def column_heating(column_state, absorb, scatter, solar_weight, cosine, surface):
    absorbing = jnp.einsum('bt,tlw->lbw', absorb, column_state, precision=lax.Precision.HIGHEST)
    scattering = scatter[None, :, None] * column_state[0][:, None, :]
    optical = absorbing + scattering
    single = single_cap * scattering / optical
    kappa_rate = 2.0 * jnp.sqrt((1.0 - single) * (1.0 - single * asymmetry))
    gamma_one = 2.0 - single * (1.0 + asymmetry)
    gamma_two = single * (1.0 - asymmetry)
    decay_one = jnp.exp(-kappa_rate * optical)
    decay_two = decay_one * decay_one
    inverse = 1.0 / (kappa_rate * (1.0 + decay_two) + gamma_one * (1.0 - decay_two))
    reflect = gamma_two * (1.0 - decay_two) * inverse
    transmit = 2.0 * kappa_rate * decay_one * inverse
    direct = jnp.exp(-optical / cosine)
    scattered = single * (1.0 - direct)
    reflect_dir = backscatter * scattered
    transmit_dir = (1.0 - backscatter) * scattered
    top_beam = jnp.broadcast_to(cosine, optical.shape[1:])

    def beam_step(beam_in, level_in):
        return (beam_in * level_in, beam_in)
    ground_beam, beam = lax.scan(beam_step, top_beam, direct)
    beam_next = jnp.concatenate([beam[1:], ground_beam[None]], axis=0)

    def upward_step(carried, level_in):
        below_albedo, below_source = carried
        layer_refl, layer_trans, refl_dir, trans_dir, beam_in = level_in
        denominator = 1.0 / (1.0 - layer_refl * below_albedo)
        albedo_new = layer_refl + layer_trans * layer_trans * below_albedo * denominator
        source_new = refl_dir * beam_in + layer_trans * (below_source + below_albedo * trans_dir * beam_in) * denominator
        return ((albedo_new, source_new), (below_albedo, below_source, denominator))
    ground = jnp.broadcast_to(surface, top_beam.shape)
    (_, top_source), (albedo_below, source_below, denoms) = lax.scan(upward_step, (ground, ground * ground_beam), (reflect, transmit, reflect_dir, transmit_dir, beam), reverse=True)

    def downward_step(carried, level_in):
        diffuse, net_above = carried
        layer_trans, layer_refl, source_b, albedo_b, denominator, trans_dir, beam_in, beam_out = level_in
        diffuse_new = (layer_trans * diffuse + layer_refl * source_b + trans_dir * beam_in) * denominator
        upward = albedo_b * diffuse_new + source_b
        net_below = beam_out + diffuse_new - upward
        return ((diffuse_new, net_below), net_above - net_below)
    zeros_flat = jnp.zeros_like(top_beam)
    _, divergence = lax.scan(downward_step, (zeros_flat, top_beam - top_source), (transmit, reflect, source_below, albedo_below, denoms, transmit_dir, beam, beam_next))
    return heat_scale * jnp.einsum('lbw,b->lw', divergence, solar_weight, precision=lax.Precision.HIGHEST)

def reference(tracers, courant_x, courant_y, sunlit, cosine_zenith, albedo, absorb, scatter, solar_weight):
    masked_y = courant_y.at[:, -1, :].set(0.0)
    flux_east = upwind(courant_x[None], tracers, jnp.roll(tracers, -1, axis=3))
    zero_row = jnp.zeros_like(tracers[:, :, :1, :])
    north_rows = jnp.concatenate([tracers[:, :, 1:, :], zero_row], axis=2)
    flux_north = upwind(masked_y[None], tracers, north_rows)
    flux_south = jnp.concatenate([zero_row, flux_north[:, :, :-1, :]], axis=2)
    tracers_next = tracers - (flux_east - jnp.roll(flux_east, 1, axis=3)) - (flux_north - flux_south)
    rows_state = jnp.moveaxis(tracers_next, 2, 0)

    def row_heating(row_data):
        column_state, cosine, surface = row_data
        return column_heating(column_state, absorb, scatter, solar_weight, cosine, surface)
    heated = lax.map(row_heating, (rows_state, cosine_zenith, albedo))
    heating = jnp.moveaxis(heated, 0, 1) * sunlit[None].astype(jnp.float32)
    return (tracers_next, heating)
```

```python
import jax
import jax.numpy as jnp
from jax import lax
from jax.experimental import pallas as pl
from jax.experimental.pallas import tpu as pltpu
from jax.sharding import PartitionSpec as P

MESH = pl.DeviceIdType.MESH
LOG2E = 1.4426950408889634
CHUNK = 16
AHEAD = 2
SHARED = 3
CY, NA, NB, SA, SB, RELAY = range(6)


def rcp(value):
    return pltpu.reciprocal(value, approx=True)


def sweep(beams, keep, nn):
    kp, kq, kd, ka, ks = keep
    levels = nn.shape[0]

    def step(level, state):
        state_new = []
        for i, (dn, beam, net) in enumerate(state):
            at = pl.ds(8 * i, 8)
            dn = kp[level, at, :] * dn + kq[level, at, :] * beam
            beam = beam * kd[level, at, :]
            below = dn * ka[level, at, :] + beam * ks[level, at, :]
            nn[level, at, :] = net - below
            state_new.append((dn, beam, below))
        return tuple(state_new)

    state = tuple((jnp.zeros_like(beam), beam, net) for beam, net in beams)
    lax.fori_loop(0, levels, step, state, unroll=8)


def summed(nn, group, i):
    levels, depth, lanes = nn.shape
    flat = nn.reshape(levels * depth, lanes)
    parts = [flat[pl.ds(group * 8 * depth + 8 * i + g, 8, stride=depth), :] for g in range(8)]
    while len(parts) > 1:
        parts = [a + b for a, b in zip(parts[::2], parts[1::2], strict=True)]
    return parts[0]


def finish(tn, heat, op, oq, od, oa, os, start_state, tn_out, heat_out, nn, full, sem):
    levels = nn.shape[0]
    rows = heat.shape[0] // levels
    moved = pltpu.make_async_copy(tn, tn_out, sem.at[0])
    moved.start()
    beams = [
        (start_state[pl.ds(16 * i, 8), :], start_state[pl.ds(16 * i + 8, 8), :]) for i in range(2)
    ]
    sweep(beams, (op, oq, od, oa, os), nn)

    def total(group, carry):
        at = pl.ds(pl.multiple_of(group * 8 * rows, 8 * rows), 8 * rows)
        full[at, :] = heat[at, :]
        for i, r in enumerate((0, rows - 1)):
            full[pl.ds(group * 8 * rows + r, 8, stride=rows), :] = summed(nn, group, i)
        return carry

    lax.fori_loop(0, levels // 8, total, 0, unroll=2)
    heated = pltpu.make_async_copy(full, heat_out, sem.at[1])
    heated.start()
    moved.wait()
    heated.wait()


def kernel(
    x4, x3, cx3, cy4, cy3, sunlit_in, cosine_in, albedo_in, absorb_in, scatter_in, weight_in,
    tn, heat, op, oq, od, oa, os, start_state,
    x, cx, cy, sunlit, cosine, albedo, absorb, scatter, weight,
    north, south, relay, pack_e, pack_w, from_e, from_w,
    cp, cq, cd, ca, cs, nn,
    load_sem, send_sem, recv_sem, lon_send, lon_recv, hop_send,
):
    tracers, levels = x4.shape[0], x4.shape[1]
    rows, lanes = x4.shape[2], x4.shape[3]
    chunks = levels // CHUNK
    lon, lat = lax.axis_index("lon"), lax.axis_index("lat")
    n_lon, n_lat = lax.axis_size("lon"), lax.axis_size("lat")
    has_n, has_s = lat < n_lat - 1, lat > 0
    to_n, to_s = (lon, lat + 1), (lon, lat - 1)
    to_e, to_w = (lax.rem(lon + 1, n_lon), lat), (lax.rem(lon + n_lon - 1, n_lon), lat)
    first, last = lat == 0, lat == n_lat - 1
    via_s, via_n = lat == 2, lat == n_lat - 3
    lo, hi = pl.ds(0, SHARED), pl.ds(SHARED, tracers - SHARED)

    pairs = (
        (x3, x), (cx3, cx), (cy3, cy), (sunlit_in, sunlit), (cosine_in, cosine),
        (albedo_in, albedo), (absorb_in, absorb), (scatter_in, scatter), (weight_in, weight),
    )
    loads = [pltpu.make_async_copy(a, b, load_sem.at[i]) for i, (a, b) in enumerate(pairs)]
    for c in loads:
        c.start()

    barrier = pltpu.get_barrier_semaphore()
    partners = [
        (None, to_e),
        (None, to_w),
        (has_n, to_n),
        (has_s, to_s),
        (first, (lon, lat + 2)),
        (via_s, (lon, lat - 2)),
        (last, (lon, lat - 2)),
        (via_n, (lon, lat + 2)),
    ]
    for here, device in partners:
        if here is None:
            pl.semaphore_signal(barrier, inc=1, device_id=device, device_id_type=MESH)
        else:

            @pl.when(here)
            def _():
                pl.semaphore_signal(barrier, inc=1, device_id=device, device_id_type=MESH)

    peers = 2
    for here, _ in partners[2:]:
        peers = peers + here.astype(jnp.int32)
    pl.semaphore_wait(barrier, peers)

    def copy(src, dst, k, kind, device):
        return pltpu.make_async_remote_copy(
            src_ref=src,
            dst_ref=dst,
            send_sem=send_sem.at[k, kind],
            recv_sem=recv_sem.at[k, kind],
            device_id=device,
            device_id_type=MESH,
        )

    def part(k):
        return pl.ds(levels - (k + 1) * CHUNK, CHUNK)

    def send_cy(k):
        return copy(cy4.at[part(k), rows - 1, :], south.at[tracers, part(k)], k, CY, to_n)

    def send_na(k):
        return copy(x4.at[lo, part(k), rows - 1, :], south.at[lo, part(k)], k, NA, to_n)

    def send_nb(k):
        return copy(x4.at[hi, part(k), rows - 1, :], south.at[hi, part(k)], k, NB, to_n)

    def send_sa(k):
        return copy(x4.at[lo, part(k), 0, :], north.at[lo, part(k)], k, SA, to_s)

    def send_sb(k):
        return copy(x4.at[hi, part(k), 0, :], north.at[hi, part(k)], k, SB, to_s)

    def send_rs(k):
        return copy(x4.at[hi, part(k), 0, :], relay.at[:, part(k)], k, RELAY, (lon, lat - 2))

    def send_rn(k):
        return copy(x4.at[hi, part(k), rows - 1, :], relay.at[:, part(k)], k, RELAY, (lon, lat + 2))

    def hop(k, dst, kind, device):
        return pltpu.make_async_remote_copy(
            src_ref=relay.at[:, part(k)],
            dst_ref=dst.at[hi, part(k)],
            send_sem=hop_send.at[k],
            recv_sem=recv_sem.at[k, kind],
            device_id=device,
            device_id_type=MESH,
        )

    direct_nb = jnp.logical_and(has_n, jnp.logical_not(via_n))
    direct_sb = jnp.logical_and(has_s, jnp.logical_not(via_s))
    detour = [(via_s, send_rs), (via_n, send_rn)]
    outgoing = [
        (has_n, send_cy),
        (has_n, send_na),
        (has_s, send_sa),
        (direct_nb, send_nb),
        (direct_sb, send_sb),
    ]

    def pass_on(k):
        @pl.when(first)
        def _():
            send_rs(k).wait_recv()
            hop(k, north, SB, to_n).start()

        @pl.when(last)
        def _():
            send_rn(k).wait_recv()
            hop(k, south, NB, to_s).start()

    def send(k, which):
        for here, make in which:

            @pl.when(here)
            def _():
                make(k).start()

    for k in range(chunks):
        send(k, detour)
    for k in range(AHEAD):
        send(k, outgoing)

    @pl.when(last)
    def _():
        north[...] = jnp.zeros_like(north)

    @pl.when(first)
    def _():
        south[...] = jnp.zeros_like(south)

    for c in loads:
        c.wait()

    lane = lax.broadcasted_iota(jnp.int32, (rows, lanes), 1)
    sub = lax.broadcasted_iota(jnp.int32, (rows, lanes), 0)

    def tile(level):
        return pl.ds(pl.multiple_of(level * rows, rows), rows)

    def pack(level, packed):
        shift = lax.rem(level + 1, lanes)
        west, east, flow = packed
        at_e, at_w = lane == level, lane == shift
        west_new, east_new = [], []
        for t in range(tracers):
            turned = pltpu.roll(x[t, tile(level), :], shift, 1)
            west_new.append(jnp.where(at_w, turned, west[t]))
            east_new.append(jnp.where(at_e, turned, east[t]))
        flow = jnp.where(at_e, pltpu.roll(cx[tile(level), :], shift, 1), flow)
        return tuple(west_new), tuple(east_new), flow

    zero = jnp.zeros((rows, lanes), jnp.float32)
    west, east, flow = lax.fori_loop(
        0, levels, pack, ((zero,) * tracers, (zero,) * tracers, zero), unroll=16
    )
    for t in range(tracers):
        pack_w[t] = west[t]
        pack_e[t] = east[t]
    pack_e[tracers] = flow
    go_w = pltpu.make_async_remote_copy(
        src_ref=pack_w, dst_ref=from_e, send_sem=lon_send.at[0], recv_sem=lon_recv.at[0],
        device_id=to_w, device_id_type=MESH,
    )
    go_e = pltpu.make_async_remote_copy(
        src_ref=pack_e, dst_ref=from_w, send_sem=lon_send.at[1], recv_sem=lon_recv.at[1],
        device_id=to_e, device_id_type=MESH,
    )
    go_w.start()
    go_e.start()
    for k in range(AHEAD):
        pass_on(k)
    go_w.wait()
    go_e.wait()
    for k in range(AHEAD, chunks):
        pass_on(k)
        send(k, outgoing)
    flow = from_w[tracers]
    for t in range(tracers):
        own = pltpu.roll(pack_w[t], lanes - 1, 1)
        from_w[t] = jnp.maximum(flow, 0.0) * from_w[t] + jnp.minimum(flow, 0.0) * own

    def advect(level, carry):
        to_first = lax.rem(2 * lanes - level, lanes)
        to_last = lax.rem(2 * lanes - 2 - level, lanes)
        here_x = cx[tile(level), :]
        here_y = jnp.where(sub == rows - 1, 0.0, cy[tile(level), :])
        xp, xm = jnp.maximum(here_x, 0.0), jnp.minimum(here_x, 0.0)
        yp, ym = jnp.maximum(here_y, 0.0), jnp.minimum(here_y, 0.0)
        for t in range(tracers):
            q = x[t, tile(level), :]
            ahead = jnp.where(
                lane == lanes - 1, pltpu.roll(from_e[t], to_last, 1), pltpu.roll(q, lanes - 1, 1)
            )
            flux_e = xp * q + xm * ahead
            flux_w = jnp.where(
                lane == 0, pltpu.roll(from_w[t], to_first, 1), pltpu.roll(flux_e, 1, 1)
            )
            flux_n = yp * q + ym * pltpu.roll(q, rows - 1, 0)
            flux_s = pltpu.roll(flux_n, 1, 0)
            tn[t, tile(level), :] = q - (flux_e - flux_w) - (flux_n - flux_s)
        return carry

    gs = absorb.shape[0]
    fold = -2.0 * LOG2E
    scat, wgt = zero, zero
    for g in range(gs):
        scat = jnp.where(sub == g, scatter[g], scat)
        wgt = jnp.where(sub == g, weight[g], wgt)
    coef = [jnp.broadcast_to(absorb[:, t : t + 1], (gs, lanes)) for t in range(tracers)]
    coef[0] = coef[0] + scat
    coef = [c * fold for c in coef]
    scat = scat * (0.9 * fold)

    def spread(ref, row):
        return jnp.broadcast_to(ref[row : row + 1, :], (gs, lanes))

    def up(which, keep, level, carry):
        half_inv = [0.5 / spread(cosine, r) for r in which]
        carry_new = []
        kp, kq, kd, ka, ks = keep
        for i, (r, half, (a, s)) in enumerate(zip(which, half_inv, carry, strict=True)):
            q = [
                jnp.broadcast_to(tn[t, pl.ds(level * rows + r, 1), :], (gs, lanes))
                for t in range(tracers)
            ]
            opt = coef[0] * q[0]
            for t in range(1, tracers):
                opt = opt + coef[t] * q[t]
            single = scat * q[0] * rcp(opt)
            square = (1.0 - single) * (1.0 - 0.85 * single)
            h = square * lax.rsqrt(square)
            e = jnp.exp2(h * opt)
            direct = jnp.exp2(opt * half)
            e2 = e * e
            u = 1.0 - e2
            inv = rcp(h * (1.0 + e2) + (1.0 - 0.925 * single) * u)
            back = 0.075 * single
            refl = back * (u * inv)
            trans = (e + e) * (h * inv)
            refl_dir = back * (1.0 - direct)
            trans_dir = (0.925 / 0.075) * refl_dir
            d = rcp(1.0 - refl * a)
            p = trans * d
            sd = s * direct
            at = pl.ds(i * gs, gs)
            kp[level, at, :] = p
            kq[level, at, :] = (refl * sd + trans_dir) * d
            kd[level, at, :] = direct
            ka[level, at, :] = 1.0 - a
            ks[level, at, :] = 1.0 - s
            a_new = refl + (trans * a) * p
            s_new = refl_dir + p * (sd + a * trans_dir)
            carry_new.append((a_new, s_new))
        return tuple(carry_new)

    def ground(which):
        return tuple((spread(albedo, r), spread(albedo, r)) for r in which)

    def top(which, carry):
        beams = []
        for r, (_, s) in zip(which, carry, strict=True):
            lit = spread(sunlit, r).astype(jnp.float32)
            beam = (4.0 * lit) * wgt * spread(cosine, r)
            beams.append((beam, beam * (1.0 - s)))
        return beams

    inner = tuple(range(1, rows - 1))
    lax.fori_loop(0, levels, advect, 0, unroll=4)
    carry = ground(inner)
    for k in range(chunks):
        start = levels - 1 - k * CHUNK
        carry = lax.fori_loop(
            0, CHUNK, lambda i, c: up(inner, (cp, cq, cd, ca, cs), start - i, c), carry, unroll=4
        )
    sweep(top(inner, carry), (cp, cq, cd, ca, cs), nn)

    def total(group, carry):
        for i, r in enumerate(inner):
            heat[pl.ds(group * 8 * rows + r, 8, stride=rows), :] = summed(nn, group, i)
        return carry

    lax.fori_loop(0, levels // 8, total, 0)

    outer = (0, rows - 1)
    carry = ground(outer)

    def every(level, row):
        return pl.ds(level * rows + row, 8, stride=rows)

    for k in range(chunks):
        for here, make in (
            (has_s, send_cy), (has_s, send_na), (has_s, send_nb), (has_n, send_sa), (has_n, send_sb),
        ):

            @pl.when(here)
            def _():
                make(k).wait_recv()

        for level in range(levels - (k + 1) * CHUNK, levels - k * CHUNK, 8):
            group = pl.ds(level, 8)
            flow_n = jnp.where(last, 0.0, cy[every(level, rows - 1), :])
            flow_s = south[tracers, group, :]
            np_, nm = jnp.maximum(flow_n, 0.0), jnp.minimum(flow_n, 0.0)
            sp, sm = jnp.maximum(flow_s, 0.0), jnp.minimum(flow_s, 0.0)
            for t in range(tracers):
                flux_n = np_ * x[t, every(level, rows - 1), :] + nm * north[t, group, :]
                flux_s = sp * south[t, group, :] + sm * x[t, every(level, 0), :]
                at_n, at_s = every(level, rows - 1), every(level, 0)
                tn[t, at_n, :] = tn[t, at_n, :] - flux_n
                tn[t, at_s, :] = tn[t, at_s, :] + flux_s
        start = levels - 1 - k * CHUNK
        carry = lax.fori_loop(
            0, CHUNK, lambda i, c: up(outer, (op, oq, od, oa, os), start - i, c), carry, unroll=4
        )
    for i, (beam, net) in enumerate(top(outer, carry)):
        start_state[pl.ds(2 * i * gs, gs), :] = beam
        start_state[pl.ds((2 * i + 1) * gs, gs), :] = net

    for k in range(chunks):
        for here, make in outgoing + detour:

            @pl.when(here)
            def _():
                make(k).wait_send()

        @pl.when(first)
        def _():
            hop(k, north, SB, to_n).wait_send()

        @pl.when(last)
        def _():
            hop(k, south, NB, to_s).wait_send()


def on_device(tracers, courant_x, courant_y, sunlit, cosine, albedo, absorb, scatter, weight):
    count, levels, rows, lanes = tracers.shape
    gs = absorb.shape[0]
    chunks = levels // CHUNK
    f32 = jnp.float32
    hbm = pl.BlockSpec(memory_space=pltpu.HBM)
    vmem = pl.BlockSpec(memory_space=pltpu.VMEM)
    dma = pltpu.SemaphoreType.DMA
    flat = levels * rows
    inner_layers = pltpu.VMEM((levels, (rows - 2) * gs, lanes), f32)
    outer_layers = pltpu.VMEM((levels, 2 * gs, lanes), f32)
    operands = (
        tracers,
        tracers.reshape(count, flat, lanes),
        courant_x.reshape(flat, lanes),
        courant_y,
        courant_y.reshape(flat, lanes),
        sunlit,
        cosine,
        albedo,
        absorb,
        scatter,
        weight,
    )
    held = pl.pallas_call(
        kernel,
        out_shape=[pltpu.VMEM((count, flat, lanes), f32), pltpu.VMEM((flat, lanes), f32)]
        + [outer_layers] * 5
        + [pltpu.VMEM((4 * gs, lanes), f32)],
        in_specs=[hbm] * 11,
        out_specs=[vmem] * 8,
        scratch_shapes=[
            pltpu.VMEM((count, flat, lanes), f32),
            pltpu.VMEM((flat, lanes), f32),
            pltpu.VMEM((flat, lanes), f32),
            pltpu.VMEM((rows, lanes), jnp.int32),
            pltpu.VMEM((rows, lanes), f32),
            pltpu.VMEM((rows, lanes), f32),
            pltpu.VMEM(absorb.shape, f32),
            pltpu.SMEM((gs,), f32),
            pltpu.SMEM((gs,), f32),
            pltpu.VMEM((count, levels, lanes), f32),
            pltpu.VMEM((count + 1, levels, lanes), f32),
            pltpu.VMEM((count - SHARED, levels, lanes), f32),
            pltpu.VMEM((count + 1, rows, lanes), f32),
            pltpu.VMEM((count, rows, lanes), f32),
            pltpu.VMEM((count, rows, lanes), f32),
            pltpu.VMEM((count + 1, rows, lanes), f32),
        ]
        + [inner_layers] * 6
        + [dma((9,)), dma((chunks, 6)), dma((chunks, 6)), dma((2,)), dma((2,)), dma((chunks,))],
        compiler_params=pltpu.CompilerParams(
            collective_id=0, has_side_effects=True, vmem_limit_bytes=36 * 2**20
        ),
        name="advect_and_heat",
    )(*[pltpu.with_memory_space_constraint(a, pltpu.HBM) for a in operands])
    moved, heating = pl.pallas_call(
        finish,
        out_shape=[pltpu.HBM((count, flat, lanes), f32), pltpu.HBM((flat, lanes), f32)],
        in_specs=[vmem] * 8,
        out_specs=[hbm] * 2,
        scratch_shapes=[outer_layers, pltpu.VMEM((flat, lanes), f32), dma((2,))],
        compiler_params=pltpu.CompilerParams(vmem_limit_bytes=8 * 2**20),
        name="finish",
    )(*[pltpu.with_memory_space_constraint(a, pltpu.VMEM) for a in held])
    return moved.reshape(tracers.shape), heating.reshape(levels, rows, lanes)


def solution(mesh):
    in_specs = (
        P(None, None, "lat", "lon"),
        P(None, "lat", "lon"),
        P(None, "lat", "lon"),
        P("lat", "lon"),
        P("lat", "lon"),
        P("lat", "lon"),
        P(),
        P(),
        P(),
    )
    out_specs = (P(None, None, "lat", "lon"), P(None, "lat", "lon"))
    return jax.shard_map(
        on_device, mesh=mesh, in_specs=in_specs, out_specs=out_specs, check_vma=False
    )
```

```python
import functools

import jax
import jax.numpy as jnp
from jax import lax
from jax.experimental import pallas as pl
from jax.experimental.pallas import tpu as pltpu
from jax.sharding import PartitionSpec as P

MESH = pl.DeviceIdType.MESH
LOG2E = 1.4426950408889634
PARTS = ((96, 32), (48, 48), (16, 32), (0, 16))
CY, NA, NB, SA, SB, RELAY = range(6)


def rcp(value):
    return pltpu.reciprocal(value, approx=True)


def sweep(beams, keep, nn):
    kp, kq, kd, ka, ks = keep
    levels = nn.shape[0]

    def step(level, state):
        state_new = []
        for i, (dn, beam, net) in enumerate(state):
            at = pl.ds(8 * i, 8)
            dn = kp[level, at, :] * dn + kq[level, at, :] * beam
            beam = beam * kd[level, at, :]
            below = dn * ka[level, at, :] + beam * ks[level, at, :]
            nn[level, at, :] = net - below
            state_new.append((dn, beam, below))
        return tuple(state_new)

    state = tuple((jnp.zeros_like(beam), beam, net) for beam, net in beams)
    lax.fori_loop(0, levels, step, state, unroll=8)


def summed(nn, group, i):
    levels, depth, lanes = nn.shape
    flat = nn.reshape(levels * depth, lanes)
    parts = [flat[pl.ds(group * 8 * depth + 8 * i + g, 8, stride=depth), :] for g in range(8)]
    while len(parts) > 1:
        parts = [a + b for a, b in zip(parts[::2], parts[1::2], strict=True)]
    return parts[0]


def finish(tn, heat, op, oq, od, oa, os, start_state, tn_out, heat_out, nn, full, sem):
    levels = nn.shape[0]
    rows = heat.shape[0] // levels
    moved = pltpu.make_async_copy(tn, tn_out, sem.at[0])
    moved.start()
    beams = [
        (start_state[pl.ds(16 * i, 8), :], start_state[pl.ds(16 * i + 8, 8), :]) for i in range(2)
    ]
    sweep(beams, (op, oq, od, oa, os), nn)

    def total(group, carry):
        at = pl.ds(pl.multiple_of(group * 8 * rows, 8 * rows), 8 * rows)
        full[at, :] = heat[at, :]
        for i, r in enumerate((0, rows - 1)):
            full[pl.ds(group * 8 * rows + r, 8, stride=rows), :] = summed(nn, group, i)
        return carry

    lax.fori_loop(0, levels // 8, total, 0, unroll=2)
    heated = pltpu.make_async_copy(full, heat_out, sem.at[1])
    heated.start()
    moved.wait()
    heated.wait()


def kernel(
    x4, x3, cx3, cy4, cy3, sunlit_in, cosine_in, albedo_in, absorb_in, scatter_in, weight_in,
    tn, heat, op, oq, od, oa, os, start_state,
    x, cx, cy, sunlit, cosine, albedo, absorb, scatter, weight,
    north, south, relay, pack_e, pack_w, from_e, from_w,
    cp, cq, cd, ca, cs, nn,
    load_sem, send_sem, recv_sem, lon_send, lon_recv, relay_recv, hop_send,
):
    tracers, levels = x4.shape[0], x4.shape[1]
    rows, lanes = x4.shape[2], x4.shape[3]
    chunks = len(PARTS)
    lon, lat = lax.axis_index("lon"), lax.axis_index("lat")
    n_lon, n_lat = lax.axis_size("lon"), lax.axis_size("lat")
    has_n, has_s = lat < n_lat - 1, lat > 0
    to_n, to_s = (lon, lat + 1), (lon, lat - 1)
    to_e, to_w = (lax.rem(lon + 1, n_lon), lat), (lax.rem(lon + n_lon - 1, n_lon), lat)
    first, last = lat == 0, lat == n_lat - 1
    middle = jnp.logical_and(has_n, has_s)
    even = lax.rem(lat, 2) == 0
    via_first = jnp.logical_and(middle, even)
    via_last = jnp.logical_and(middle, jnp.logical_not(even))
    slots = relay.shape[0]
    slot = lax.div(lat - 1, 2)

    def direct(k):
        return pl.ds(0, tracers - 1 - k % 2)

    def shared(k):
        return pl.ds(tracers - 1 - k % 2, 1 + k % 2)

    pairs = (
        (cx3, cx), *[(x3.at[t], x.at[t]) for t in range(tracers)],
        (cy3, cy), (sunlit_in, sunlit), (cosine_in, cosine), (albedo_in, albedo),
        (absorb_in, absorb), (scatter_in, scatter), (weight_in, weight),
    )
    loads = [pltpu.make_async_copy(a, b, load_sem.at[i]) for i, (a, b) in enumerate(pairs)]
    for c in loads:
        c.start()

    barrier = pltpu.get_barrier_semaphore()
    partners = [
        (None, to_e),
        (None, to_w),
        (has_n, to_n),
        (has_s, to_s),
        (jnp.logical_and(middle, lat > 1), (lon, 0)),
        (jnp.logical_and(middle, lat < n_lat - 2), (lon, n_lat - 1)),
    ]
    for other in range(1, n_lat - 1):
        if other > 1:
            partners.append((first, (lon, other)))
        if other < n_lat - 2:
            partners.append((last, (lon, other)))
    for here, device in partners:
        if here is None:
            pl.semaphore_signal(barrier, inc=1, device_id=device, device_id_type=MESH)
        else:

            @pl.when(here)
            def _():
                pl.semaphore_signal(barrier, inc=1, device_id=device, device_id_type=MESH)

    peers = 2
    for here, _ in partners[2:]:
        peers = peers + here.astype(jnp.int32)
    def copy(src, dst, k, kind, device):
        return pltpu.make_async_remote_copy(
            src_ref=src,
            dst_ref=dst,
            send_sem=send_sem.at[k, kind],
            recv_sem=recv_sem.at[k, kind],
            device_id=device,
            device_id_type=MESH,
        )

    def part(k):
        return pl.ds(*PARTS[k])

    def send_cy(k):
        return copy(cy4.at[part(k), rows - 1, :], south.at[tracers, part(k)], k, CY, to_n)

    def rows_to_n(k, planes, kind):
        src, dst = x4.at[planes, part(k), rows - 1, :], south.at[planes, part(k)]
        return copy(src, dst, k, kind, to_n)

    def rows_to_s(k, planes, kind):
        src, dst = x4.at[planes, part(k), 0, :], north.at[planes, part(k)]
        return copy(src, dst, k, kind, to_s)

    def send_na(k):
        return rows_to_n(k, direct(k), NA)

    def send_nb(k):
        return rows_to_n(k, shared(k), NB)

    def send_n(k):
        return rows_to_n(k, pl.ds(0, tracers), NA)

    def send_sa(k):
        return rows_to_s(k, direct(k), SA)

    def send_sb(k):
        return rows_to_s(k, shared(k), SB)

    def send_s(k):
        return rows_to_s(k, pl.ds(0, tracers), SA)

    def detour_row(k, row, at, to):
        return pltpu.make_async_remote_copy(
            src_ref=x4.at[shared(k), part(k), row, :],
            dst_ref=relay.at[at, pl.ds(0, 1 + k % 2), part(k)],
            send_sem=send_sem.at[k, RELAY],
            recv_sem=relay_recv.at[k, at],
            device_id=(lon, to),
            device_id_type=MESH,
        )

    def send_rs(k):
        return detour_row(k, 0, slot, 0)

    def send_rn(k):
        return detour_row(k, rows - 1, slot, n_lat - 1)

    def hop(k, at, dst, kind, to):
        return pltpu.make_async_remote_copy(
            src_ref=relay.at[at, pl.ds(0, 1 + k % 2), part(k)],
            dst_ref=dst.at[shared(k), part(k)],
            send_sem=hop_send.at[k, at],
            recv_sem=recv_sem.at[k, kind],
            device_id=(lon, to),
            device_id_type=MESH,
        )

    def hop_s(k, at):
        return hop(k, at, north, SB, 2 * at + 1)

    def hop_n(k, at):
        return hop(k, at, south, NB, 2 * at + 2)

    detour = [(via_first, send_rs), (via_last, send_rn)]
    outgoing = [
        (has_n, send_cy),
        (jnp.logical_and(has_n, jnp.logical_not(via_last)), send_n),
        (via_last, send_na),
        (jnp.logical_and(has_s, jnp.logical_not(via_first)), send_s),
        (via_first, send_sa),
    ]
    whole_s, split_s = jnp.logical_and(has_s, jnp.logical_not(even)), jnp.logical_and(has_s, even)
    whole_n, split_n = jnp.logical_and(has_n, even), jnp.logical_and(has_n, jnp.logical_not(even))
    incoming = [
        (has_s, send_cy),
        (whole_s, send_n),
        (split_s, send_na),
        (split_s, send_nb),
        (whole_n, send_s),
        (split_n, send_sa),
        (split_n, send_sb),
    ]

    def pass_on(k):
        for at in range(slots):

            @pl.when(first)
            def _():
                detour_row(k, 0, at, 0).wait_recv()
                hop_s(k, at).start()

            @pl.when(last)
            def _():
                detour_row(k, rows - 1, at, n_lat - 1).wait_recv()
                hop_n(k, at).start()

    def send(k, which):
        for here, make in which:

            @pl.when(here)
            def _():
                make(k).start()

    @pl.when(last)
    def _():
        north[...] = jnp.zeros_like(north)

    @pl.when(first)
    def _():
        south[...] = jnp.zeros_like(south)

    lane = lax.broadcasted_iota(jnp.int32, (rows, lanes), 1)
    sub = lax.broadcasted_iota(jnp.int32, (rows, lanes), 0)

    def tile(level):
        return pl.ds(pl.multiple_of(level * rows, rows), rows)

    def pack(fields, level, packed):
        shift = lax.rem(level + 1, lanes)
        at_e, at_w = lane == level, lane == shift
        packed_new = []
        for field, (west, east) in zip(fields, packed, strict=True):
            turned = pltpu.roll(field[tile(level), :], shift, 1)
            packed_new.append((jnp.where(at_w, turned, west), jnp.where(at_e, turned, east)))
        return tuple(packed_new)

    zero = jnp.zeros((rows, lanes), jnp.float32)
    loads[0].wait()
    for t in range(0, tracers, 2):
        loads[1 + t].wait()
        loads[2 + t].wait()
        fields = [x.at[t], x.at[t + 1]] + ([cx] if t == 0 else [])
        packed = lax.fori_loop(
            0,
            levels,
            functools.partial(pack, fields),
            ((zero, zero),) * len(fields),
            unroll=32,
        )
        for u, (west, east) in enumerate(packed[:2]):
            pack_w[t + u] = west
            pack_e[t + u] = east
        if t == 0:
            pack_e[tracers] = packed[2][1]
    go_w = pltpu.make_async_remote_copy(
        src_ref=pack_w, dst_ref=from_e, send_sem=lon_send.at[0], recv_sem=lon_recv.at[0],
        device_id=to_w, device_id_type=MESH,
    )
    go_e = pltpu.make_async_remote_copy(
        src_ref=pack_e, dst_ref=from_w, send_sem=lon_send.at[1], recv_sem=lon_recv.at[1],
        device_id=to_e, device_id_type=MESH,
    )
    pl.semaphore_wait(barrier, peers)
    go_w.start()
    go_e.start()
    for k in range(chunks):
        send(k, detour)
    for k in range(chunks):
        send(k, outgoing)
    for c in loads[1 + tracers :]:
        c.wait()
    go_w.wait()
    go_e.wait()
    for k in range(chunks):
        pass_on(k)
    flow = from_w[tracers]
    for t in range(tracers):
        own = pltpu.roll(pack_w[t], lanes - 1, 1)
        from_w[t] = jnp.maximum(flow, 0.0) * from_w[t] + jnp.minimum(flow, 0.0) * own

    def advect(level, carry):
        to_first = lax.rem(2 * lanes - level, lanes)
        to_last = lax.rem(2 * lanes - 2 - level, lanes)
        here_x = cx[tile(level), :]
        here_y = jnp.where(sub == rows - 1, 0.0, cy[tile(level), :])
        xp, xm = jnp.maximum(here_x, 0.0), jnp.minimum(here_x, 0.0)
        yp, ym = jnp.maximum(here_y, 0.0), jnp.minimum(here_y, 0.0)
        for t in range(tracers):
            q = x[t, tile(level), :]
            ahead = jnp.where(
                lane == lanes - 1, pltpu.roll(from_e[t], to_last, 1), pltpu.roll(q, lanes - 1, 1)
            )
            flux_e = xp * q + xm * ahead
            flux_w = jnp.where(
                lane == 0, pltpu.roll(from_w[t], to_first, 1), pltpu.roll(flux_e, 1, 1)
            )
            flux_n = yp * q + ym * pltpu.roll(q, rows - 1, 0)
            flux_s = pltpu.roll(flux_n, 1, 0)
            tn[t, tile(level), :] = q - (flux_e - flux_w) - (flux_n - flux_s)
        return carry

    gs = absorb.shape[0]
    fold = -2.0 * LOG2E
    scat, wgt = zero, zero
    for g in range(gs):
        scat = jnp.where(sub == g, scatter[g], scat)
        wgt = jnp.where(sub == g, weight[g], wgt)
    coef = [jnp.broadcast_to(absorb[:, t : t + 1], (gs, lanes)) for t in range(tracers)]
    coef[0] = coef[0] + scat
    coef = [c * fold for c in coef]
    scat = scat * (0.9 * fold)

    def spread(ref, row):
        return jnp.broadcast_to(ref[row : row + 1, :], (gs, lanes))

    def up(which, keep, level, carry):
        half_inv = [0.5 / spread(cosine, r) for r in which]
        carry_new = []
        kp, kq, kd, ka, ks = keep
        for i, (r, half, (a, s)) in enumerate(zip(which, half_inv, carry, strict=True)):
            q = [
                jnp.broadcast_to(tn[t, pl.ds(level * rows + r, 1), :], (gs, lanes))
                for t in range(tracers)
            ]
            opt = coef[0] * q[0]
            for t in range(1, tracers):
                opt = opt + coef[t] * q[t]
            single = scat * q[0] * rcp(opt)
            square = (1.0 - single) * (1.0 - 0.85 * single)
            h = square * lax.rsqrt(square)
            e = jnp.exp2(h * opt)
            direct = jnp.exp2(opt * half)
            e2 = e * e
            u = 1.0 - e2
            inv = rcp(h * (1.0 + e2) + (1.0 - 0.925 * single) * u)
            back = 0.075 * single
            refl = back * (u * inv)
            trans = (e + e) * (h * inv)
            refl_dir = back * (1.0 - direct)
            trans_dir = (0.925 / 0.075) * refl_dir
            d = rcp(1.0 - refl * a)
            p = trans * d
            sd = s * direct
            at = pl.ds(i * gs, gs)
            kp[level, at, :] = p
            kq[level, at, :] = (refl * sd + trans_dir) * d
            kd[level, at, :] = direct
            ka[level, at, :] = 1.0 - a
            ks[level, at, :] = 1.0 - s
            a_new = refl + (trans * a) * p
            s_new = refl_dir + p * (sd + a * trans_dir)
            carry_new.append((a_new, s_new))
        return tuple(carry_new)

    def ground(which):
        return tuple((spread(albedo, r), spread(albedo, r)) for r in which)

    def top(which, carry):
        beams = []
        for r, (_, s) in zip(which, carry, strict=True):
            lit = spread(sunlit, r).astype(jnp.float32)
            beam = (4.0 * lit) * wgt * spread(cosine, r)
            beams.append((beam, beam * (1.0 - s)))
        return beams

    inner = tuple(range(1, rows - 1))
    lax.fori_loop(0, levels, advect, 0, unroll=4)
    carry = ground(inner)
    carry = lax.fori_loop(
        0, levels, lambda i, c: up(inner, (cp, cq, cd, ca, cs), levels - 1 - i, c), carry, unroll=4
    )
    sweep(top(inner, carry), (cp, cq, cd, ca, cs), nn)

    def total(group, carry):
        for i, r in enumerate(inner):
            heat[pl.ds(group * 8 * rows + r, 8, stride=rows), :] = summed(nn, group, i)
        return carry

    lax.fori_loop(0, levels // 8, total, 0)

    outer = (0, rows - 1)
    carry = ground(outer)

    def every(level, row):
        return pl.ds(level * rows + row, 8, stride=rows)

    for k, (low, count) in enumerate(PARTS):
        for here, make in incoming:

            @pl.when(here)
            def _():
                make(k).wait_recv()

        def edges(i, c):
            level = low + 8 * i
            group = pl.ds(pl.multiple_of(level, 8), 8)
            flow_n = jnp.where(last, 0.0, cy[every(level, rows - 1), :])
            flow_s = south[tracers, group, :]
            np_, nm = jnp.maximum(flow_n, 0.0), jnp.minimum(flow_n, 0.0)
            sp, sm = jnp.maximum(flow_s, 0.0), jnp.minimum(flow_s, 0.0)
            for t in range(tracers):
                flux_n = np_ * x[t, every(level, rows - 1), :] + nm * north[t, group, :]
                flux_s = sp * south[t, group, :] + sm * x[t, every(level, 0), :]
                at_n, at_s = every(level, rows - 1), every(level, 0)
                tn[t, at_n, :] = tn[t, at_n, :] - flux_n
                tn[t, at_s, :] = tn[t, at_s, :] + flux_s
            return c

        lax.fori_loop(0, count // 8, edges, 0, unroll=2)
        start = low + count - 1
        carry = lax.fori_loop(
            0, count, lambda i, c: up(outer, (op, oq, od, oa, os), start - i, c), carry, unroll=4
        )
    for i, (beam, net) in enumerate(top(outer, carry)):
        start_state[pl.ds(2 * i * gs, gs), :] = beam
        start_state[pl.ds((2 * i + 1) * gs, gs), :] = net

    for k in range(chunks):
        for here, make in outgoing + detour:

            @pl.when(here)
            def _():
                make(k).wait_send()

        for at in range(slots):

            @pl.when(first)
            def _():
                hop_s(k, at).wait_send()

            @pl.when(last)
            def _():
                hop_n(k, at).wait_send()


def on_device(tracers, courant_x, courant_y, sunlit, cosine, albedo, absorb, scatter, weight):
    count, levels, rows, lanes = tracers.shape
    gs = absorb.shape[0]
    chunks = len(PARTS)
    slots = lax.axis_size("lat") // 2 - 1
    f32 = jnp.float32
    hbm = pl.BlockSpec(memory_space=pltpu.HBM)
    vmem = pl.BlockSpec(memory_space=pltpu.VMEM)
    dma = pltpu.SemaphoreType.DMA
    flat = levels * rows
    inner_layers = pltpu.VMEM((levels, (rows - 2) * gs, lanes), f32)
    outer_layers = pltpu.VMEM((levels, 2 * gs, lanes), f32)
    operands = (
        tracers,
        tracers.reshape(count, flat, lanes),
        courant_x.reshape(flat, lanes),
        courant_y,
        courant_y.reshape(flat, lanes),
        sunlit,
        cosine,
        albedo,
        absorb,
        scatter,
        weight,
    )
    held = pl.pallas_call(
        kernel,
        out_shape=[pltpu.VMEM((count, flat, lanes), f32), pltpu.VMEM((flat, lanes), f32)]
        + [outer_layers] * 5
        + [pltpu.VMEM((4 * gs, lanes), f32)],
        in_specs=[hbm] * 11,
        out_specs=[vmem] * 8,
        scratch_shapes=[
            pltpu.VMEM((count, flat, lanes), f32),
            pltpu.VMEM((flat, lanes), f32),
            pltpu.VMEM((flat, lanes), f32),
            pltpu.VMEM((rows, lanes), jnp.int32),
            pltpu.VMEM((rows, lanes), f32),
            pltpu.VMEM((rows, lanes), f32),
            pltpu.VMEM(absorb.shape, f32),
            pltpu.SMEM((gs,), f32),
            pltpu.SMEM((gs,), f32),
            pltpu.VMEM((count, levels, lanes), f32),
            pltpu.VMEM((count + 1, levels, lanes), f32),
            pltpu.VMEM((slots, 2, levels, lanes), f32),
            pltpu.VMEM((count + 1, rows, lanes), f32),
            pltpu.VMEM((count, rows, lanes), f32),
            pltpu.VMEM((count, rows, lanes), f32),
            pltpu.VMEM((count + 1, rows, lanes), f32),
        ]
        + [inner_layers] * 6
        + [dma((count + 8,)), dma((chunks, 6)), dma((chunks, 6)), dma((2,)), dma((2,))]
        + [dma((chunks, slots)), dma((chunks, slots))],
        compiler_params=pltpu.CompilerParams(
            collective_id=0, has_side_effects=True, vmem_limit_bytes=36 * 2**20
        ),
        name="advect_and_heat",
    )(*[pltpu.with_memory_space_constraint(a, pltpu.HBM) for a in operands])
    moved, heating = pl.pallas_call(
        finish,
        out_shape=[pltpu.HBM((count, flat, lanes), f32), pltpu.HBM((flat, lanes), f32)],
        in_specs=[vmem] * 8,
        out_specs=[hbm] * 2,
        scratch_shapes=[outer_layers, pltpu.VMEM((flat, lanes), f32), dma((2,))],
        compiler_params=pltpu.CompilerParams(vmem_limit_bytes=8 * 2**20),
        name="finish",
    )(*[pltpu.with_memory_space_constraint(a, pltpu.VMEM) for a in held])
    return moved.reshape(tracers.shape), heating.reshape(levels, rows, lanes)


def solution(mesh):
    in_specs = (
        P(None, None, "lat", "lon"),
        P(None, "lat", "lon"),
        P(None, "lat", "lon"),
        P("lat", "lon"),
        P("lat", "lon"),
        P("lat", "lon"),
        P(),
        P(),
        P(),
    )
    out_specs = (P(None, None, "lat", "lon"), P(None, "lat", "lon"))
    return jax.shard_map(
        on_device, mesh=mesh, in_specs=in_specs, out_specs=out_specs, check_vma=False
    )
```

```python
import functools

import jax
import jax.numpy as jnp
from jax import lax
from jax.experimental import pallas as pl
from jax.experimental.pallas import tpu as pltpu
from jax.sharding import PartitionSpec as P

MESH = pl.DeviceIdType.MESH
LOG2E = 1.4426950408889634
PARTS = ((96, 32), (48, 48), (16, 32), (0, 16))
NA, NB, SA, SB, RELAY = range(5)


def rcp(value):
    return pltpu.reciprocal(value, approx=True)


def sweep(beams, keep, nn):
    kp, kq, kd, ka, ks = keep
    levels = nn.shape[0]

    def step(level, state):
        state_new = []
        for i, (dn, beam, net) in enumerate(state):
            at = pl.ds(8 * i, 8)
            dn = kp[level, at, :] * dn + kq[level, at, :] * beam
            beam = beam * kd[level, at, :]
            below = dn * ka[level, at, :] + beam * ks[level, at, :]
            nn[level, at, :] = net - below
            state_new.append((dn, beam, below))
        return tuple(state_new)

    state = tuple((jnp.zeros_like(beam), beam, net) for beam, net in beams)
    lax.fori_loop(0, levels, step, state, unroll=8)


def summed(nn, group, i):
    levels, depth, lanes = nn.shape
    flat = nn.reshape(levels * depth, lanes)
    parts = [flat[pl.ds(group * 8 * depth + 8 * i + g, 8, stride=depth), :] for g in range(8)]
    while len(parts) > 1:
        parts = [a + b for a, b in zip(parts[::2], parts[1::2], strict=True)]
    return parts[0]


def finish(tn, heat, op, oq, od, oa, os, start_state, tn_out, heat_out, nn, full, sem):
    levels = nn.shape[0]
    rows = heat.shape[0] // levels
    moved = pltpu.make_async_copy(tn, tn_out, sem.at[0])
    moved.start()
    beams = [
        (start_state[pl.ds(16 * i, 8), :], start_state[pl.ds(16 * i + 8, 8), :]) for i in range(2)
    ]
    sweep(beams, (op, oq, od, oa, os), nn)

    def total(group, carry):
        at = pl.ds(pl.multiple_of(group * 8 * rows, 8 * rows), 8 * rows)
        full[at, :] = heat[at, :]
        for i, r in enumerate((0, rows - 1)):
            full[pl.ds(group * 8 * rows + r, 8, stride=rows), :] = summed(nn, group, i)
        return carry

    lax.fori_loop(0, levels // 8, total, 0, unroll=2)
    heated = pltpu.make_async_copy(full, heat_out, sem.at[1])
    heated.start()
    moved.wait()
    heated.wait()


def kernel(
    x4, x3, cx3, cy3, sunlit_in, cosine_in, albedo_in, absorb_in, scatter_in, weight_in,
    tn, heat, op, oq, od, oa, os, start_state,
    x, cx, cy, sunlit, cosine, albedo, absorb, scatter, weight,
    rows_n, north, south, relay, pack_e, pack_w, from_e, from_w,
    cp, cq, cd, ca, cs, nn,
    load_sem, send_sem, recv_sem, lon_send, lon_recv, relay_recv, hop_send,
):
    tracers, levels = x4.shape[0], x4.shape[1]
    rows, lanes = x4.shape[2], x4.shape[3]
    chunks = len(PARTS)
    lon, lat = lax.axis_index("lon"), lax.axis_index("lat")
    n_lon, n_lat = lax.axis_size("lon"), lax.axis_size("lat")
    has_n, has_s = lat < n_lat - 1, lat > 0
    to_n, to_s = (lon, lat + 1), (lon, lat - 1)
    to_e, to_w = (lax.rem(lon + 1, n_lon), lat), (lax.rem(lon + n_lon - 1, n_lon), lat)
    first, last = lat == 0, lat == n_lat - 1
    middle = jnp.logical_and(has_n, has_s)
    even = lax.rem(lat, 2) == 0
    via_first = jnp.logical_and(middle, even)
    via_last = jnp.logical_and(middle, jnp.logical_not(even))
    slots = relay.shape[0]
    slot = lax.div(lat - 1, 2)

    def direct(k):
        return pl.ds(0, tracers - 1 - k % 2)

    def shared(k):
        return pl.ds(tracers - 1 - k % 2, 1 + k % 2)

    pairs = (
        (cx3, cx), *[(x3.at[t], x.at[t]) for t in range(tracers)],
        (cy3, cy), (sunlit_in, sunlit), (cosine_in, cosine), (albedo_in, albedo),
        (absorb_in, absorb), (scatter_in, scatter), (weight_in, weight),
    )
    loads = [pltpu.make_async_copy(a, b, load_sem.at[i]) for i, (a, b) in enumerate(pairs)]
    for c in loads:
        c.start()

    barrier = pltpu.get_barrier_semaphore()
    partners = [
        (None, to_e),
        (None, to_w),
        (has_n, to_n),
        (has_s, to_s),
        (jnp.logical_and(middle, lat > 1), (lon, 0)),
        (jnp.logical_and(middle, lat < n_lat - 2), (lon, n_lat - 1)),
    ]
    for other in range(1, n_lat - 1):
        if other > 1:
            partners.append((first, (lon, other)))
        if other < n_lat - 2:
            partners.append((last, (lon, other)))
    for here, device in partners:
        if here is None:
            pl.semaphore_signal(barrier, inc=1, device_id=device, device_id_type=MESH)
        else:

            @pl.when(here)
            def _():
                pl.semaphore_signal(barrier, inc=1, device_id=device, device_id_type=MESH)

    peers = 2
    for here, _ in partners[2:]:
        peers = peers + here.astype(jnp.int32)
    def copy(src, dst, k, kind, device):
        return pltpu.make_async_remote_copy(
            src_ref=src,
            dst_ref=dst,
            send_sem=send_sem.at[k, kind],
            recv_sem=recv_sem.at[k, kind],
            device_id=device,
            device_id_type=MESH,
        )

    def part(k):
        return pl.ds(*PARTS[k])

    def rows_to_n(k, planes, kind):
        src, dst = rows_n.at[planes, part(k)], south.at[planes, part(k)]
        return copy(src, dst, k, kind, to_n)

    def rows_to_s(k, planes, kind):
        src, dst = x4.at[planes, part(k), 0, :], north.at[planes, part(k)]
        return copy(src, dst, k, kind, to_s)

    def send_na(k):
        return rows_to_n(k, direct(k), NA)

    def send_nb(k):
        return rows_to_n(k, shared(k), NB)

    def send_n(k):
        return rows_to_n(k, pl.ds(0, tracers), NA)

    def send_sa(k):
        return rows_to_s(k, direct(k), SA)

    def send_sb(k):
        return rows_to_s(k, shared(k), SB)

    def send_s(k):
        return rows_to_s(k, pl.ds(0, tracers), SA)

    def detour_row(k, planes_of, at, to):
        return pltpu.make_async_remote_copy(
            src_ref=planes_of,
            dst_ref=relay.at[at, pl.ds(0, 1 + k % 2), part(k)],
            send_sem=send_sem.at[k, RELAY],
            recv_sem=relay_recv.at[k, at],
            device_id=(lon, to),
            device_id_type=MESH,
        )

    def send_rs(k):
        return detour_row(k, x4.at[shared(k), part(k), 0, :], slot, 0)

    def send_rn(k):
        return detour_row(k, rows_n.at[shared(k), part(k)], slot, n_lat - 1)

    def hop(k, at, dst, kind, to):
        return pltpu.make_async_remote_copy(
            src_ref=relay.at[at, pl.ds(0, 1 + k % 2), part(k)],
            dst_ref=dst.at[shared(k), part(k)],
            send_sem=hop_send.at[k, at],
            recv_sem=recv_sem.at[k, kind],
            device_id=(lon, to),
            device_id_type=MESH,
        )

    def hop_s(k, at):
        return hop(k, at, north, SB, 2 * at + 1)

    def hop_n(k, at):
        return hop(k, at, south, NB, 2 * at + 2)

    detour_s, detour_n = [(via_first, send_rs)], [(via_last, send_rn)]
    northward = [
        (jnp.logical_and(has_n, jnp.logical_not(via_last)), send_n),
        (via_last, send_na),
    ]
    southward = [
        (jnp.logical_and(has_s, jnp.logical_not(via_first)), send_s),
        (via_first, send_sa),
    ]
    whole_s, split_s = jnp.logical_and(has_s, jnp.logical_not(even)), jnp.logical_and(has_s, even)
    whole_n, split_n = jnp.logical_and(has_n, even), jnp.logical_and(has_n, jnp.logical_not(even))
    incoming = [
        (whole_s, send_n),
        (split_s, send_na),
        (split_s, send_nb),
        (whole_n, send_s),
        (split_n, send_sa),
        (split_n, send_sb),
    ]

    def pass_on(k):
        for at in range(slots):

            @pl.when(first)
            def _():
                detour_row(k, x4.at[shared(k), part(k), 0, :], at, 0).wait_recv()
                hop_s(k, at).start()

            @pl.when(last)
            def _():
                detour_row(k, rows_n.at[shared(k), part(k)], at, n_lat - 1).wait_recv()
                hop_n(k, at).start()

    def send(k, which):
        for here, make in which:

            @pl.when(here)
            def _():
                make(k).start()

    @pl.when(last)
    def _():
        north[...] = jnp.zeros_like(north)

    @pl.when(first)
    def _():
        south[...] = jnp.zeros_like(south)

    lane = lax.broadcasted_iota(jnp.int32, (rows, lanes), 1)
    sub = lax.broadcasted_iota(jnp.int32, (rows, lanes), 0)

    def tile(level):
        return pl.ds(pl.multiple_of(level * rows, rows), rows)

    def every(level, row):
        return pl.ds(level * rows + row, 8, stride=rows)

    def pack(fields, level, packed):
        shift = lax.rem(level + 1, lanes)
        at_e, at_w = lane == level, lane == shift
        packed_new = []
        for field, (west, east) in zip(fields, packed, strict=True):
            turned = pltpu.roll(field[tile(level), :], shift, 1)
            packed_new.append((jnp.where(at_w, turned, west), jnp.where(at_e, turned, east)))
        return tuple(packed_new)

    zero = jnp.zeros((rows, lanes), jnp.float32)
    loads[0].wait()
    for t in range(0, tracers, 2):
        loads[1 + t].wait()
        loads[2 + t].wait()
        fields = [x.at[t], x.at[t + 1]] + ([cx] if t == 0 else [])
        packed = lax.fori_loop(
            0,
            levels,
            functools.partial(pack, fields),
            ((zero, zero),) * len(fields),
            unroll=32,
        )
        for u, (west, east) in enumerate(packed[:2]):
            pack_w[t + u] = west
            pack_e[t + u] = east
        if t == 0:
            pack_e[tracers] = packed[2][1]
    go_w = pltpu.make_async_remote_copy(
        src_ref=pack_w, dst_ref=from_e, send_sem=lon_send.at[0], recv_sem=lon_recv.at[0],
        device_id=to_w, device_id_type=MESH,
    )
    go_e = pltpu.make_async_remote_copy(
        src_ref=pack_e, dst_ref=from_w, send_sem=lon_send.at[1], recv_sem=lon_recv.at[1],
        device_id=to_e, device_id_type=MESH,
    )
    pl.semaphore_wait(barrier, peers)
    go_w.start()
    go_e.start()
    for k in range(chunks):
        send(k, detour_s)
    send(0, southward)
    for c in loads[1 + tracers :]:
        c.wait()

    def gather(group, carry):
        at = pl.ds(pl.multiple_of(group * 8, 8), 8)
        flow = cy[every(group * 8, rows - 1), :]
        inward = jnp.maximum(flow, 0.0)
        for t in range(tracers):
            share = inward * x[t, every(group * 8, rows - 1), :]
            rows_n[t, at, :] = jnp.where(flow < 0.0, flow, share) if t == 0 else share
        return carry

    lax.fori_loop(0, levels // 8, gather, 0, unroll=4)
    for k in range(chunks):
        send(k, detour_n)
    send(0, northward)
    for k in range(1, chunks):
        send(k, southward)
        send(k, northward)
    go_w.wait()
    go_e.wait()
    for k in range(chunks):
        pass_on(k)
    flow = from_w[tracers]
    for t in range(tracers):
        own = pltpu.roll(pack_w[t], lanes - 1, 1)
        from_w[t] = jnp.maximum(flow, 0.0) * from_w[t] + jnp.minimum(flow, 0.0) * own

    def advect(level, carry):
        to_first = lax.rem(2 * lanes - level, lanes)
        to_last = lax.rem(2 * lanes - 2 - level, lanes)
        here_x = cx[tile(level), :]
        here_y = jnp.where(sub == rows - 1, 0.0, cy[tile(level), :])
        xp, xm = jnp.maximum(here_x, 0.0), jnp.minimum(here_x, 0.0)
        yp, ym = jnp.maximum(here_y, 0.0), jnp.minimum(here_y, 0.0)
        for t in range(tracers):
            q = x[t, tile(level), :]
            ahead = jnp.where(
                lane == lanes - 1, pltpu.roll(from_e[t], to_last, 1), pltpu.roll(q, lanes - 1, 1)
            )
            flux_e = xp * q + xm * ahead
            flux_w = jnp.where(
                lane == 0, pltpu.roll(from_w[t], to_first, 1), pltpu.roll(flux_e, 1, 1)
            )
            flux_n = yp * q + ym * pltpu.roll(q, rows - 1, 0)
            flux_s = pltpu.roll(flux_n, 1, 0)
            tn[t, tile(level), :] = q - (flux_e - flux_w) - (flux_n - flux_s)
        return carry

    gs = absorb.shape[0]
    fold = -2.0 * LOG2E
    scat, wgt = zero, zero
    for g in range(gs):
        scat = jnp.where(sub == g, scatter[g], scat)
        wgt = jnp.where(sub == g, weight[g], wgt)
    coef = [jnp.broadcast_to(absorb[:, t : t + 1], (gs, lanes)) for t in range(tracers)]
    coef[0] = coef[0] + scat
    coef = [c * fold for c in coef]
    scat = scat * (0.9 * fold)

    def spread(ref, row):
        return jnp.broadcast_to(ref[row : row + 1, :], (gs, lanes))

    def up(which, keep, level, carry):
        half_inv = [0.5 / spread(cosine, r) for r in which]
        carry_new = []
        kp, kq, kd, ka, ks = keep
        for i, (r, half, (a, s)) in enumerate(zip(which, half_inv, carry, strict=True)):
            q = [
                jnp.broadcast_to(tn[t, pl.ds(level * rows + r, 1), :], (gs, lanes))
                for t in range(tracers)
            ]
            opt = coef[0] * q[0]
            for t in range(1, tracers):
                opt = opt + coef[t] * q[t]
            single = scat * q[0] * rcp(opt)
            square = (1.0 - single) * (1.0 - 0.85 * single)
            h = square * lax.rsqrt(square)
            e = jnp.exp2(h * opt)
            direct = jnp.exp2(opt * half)
            e2 = e * e
            u = 1.0 - e2
            inv = rcp(h * (1.0 + e2) + (1.0 - 0.925 * single) * u)
            back = 0.075 * single
            refl = back * (u * inv)
            trans = (e + e) * (h * inv)
            refl_dir = back * (1.0 - direct)
            trans_dir = (0.925 / 0.075) * refl_dir
            d = rcp(1.0 - refl * a)
            p = trans * d
            sd = s * direct
            at = pl.ds(i * gs, gs)
            kp[level, at, :] = p
            kq[level, at, :] = (refl * sd + trans_dir) * d
            kd[level, at, :] = direct
            ka[level, at, :] = 1.0 - a
            ks[level, at, :] = 1.0 - s
            a_new = refl + (trans * a) * p
            s_new = refl_dir + p * (sd + a * trans_dir)
            carry_new.append((a_new, s_new))
        return tuple(carry_new)

    def ground(which):
        return tuple((spread(albedo, r), spread(albedo, r)) for r in which)

    def top(which, carry):
        beams = []
        for r, (_, s) in zip(which, carry, strict=True):
            lit = spread(sunlit, r).astype(jnp.float32)
            beam = (4.0 * lit) * wgt * spread(cosine, r)
            beams.append((beam, beam * (1.0 - s)))
        return beams

    inner = tuple(range(1, rows - 1))
    lax.fori_loop(0, levels, advect, 0, unroll=4)
    carry = ground(inner)
    carry = lax.fori_loop(
        0, levels, lambda i, c: up(inner, (cp, cq, cd, ca, cs), levels - 1 - i, c), carry, unroll=4
    )
    sweep(top(inner, carry), (cp, cq, cd, ca, cs), nn)

    def total(group, carry):
        for i, r in enumerate(inner):
            heat[pl.ds(group * 8 * rows + r, 8, stride=rows), :] = summed(nn, group, i)
        return carry

    lax.fori_loop(0, levels // 8, total, 0)

    outer = (0, rows - 1)
    carry = ground(outer)

    for k, (low, count) in enumerate(PARTS):
        for here, make in incoming:

            @pl.when(here)
            def _():
                make(k).wait_recv()

        def edges(i, c):
            level = low + 8 * i
            group = pl.ds(pl.multiple_of(level, 8), 8)
            flow_n = jnp.where(last, 0.0, cy[every(level, rows - 1), :])
            flow_s = south[0, group, :]
            np_, nm = jnp.maximum(flow_n, 0.0), jnp.minimum(flow_n, 0.0)
            sm = jnp.minimum(flow_s, 0.0)
            for t in range(tracers):
                flux_n = np_ * x[t, every(level, rows - 1), :] + nm * north[t, group, :]
                share = south[t, group, :] if t else jnp.maximum(flow_s, 0.0)
                flux_s = share + sm * x[t, every(level, 0), :]
                at_n, at_s = every(level, rows - 1), every(level, 0)
                tn[t, at_n, :] = tn[t, at_n, :] - flux_n
                tn[t, at_s, :] = tn[t, at_s, :] + flux_s
            return c

        lax.fori_loop(0, count // 8, edges, 0, unroll=2)
        start = low + count - 1
        carry = lax.fori_loop(
            0, count, lambda i, c: up(outer, (op, oq, od, oa, os), start - i, c), carry, unroll=4
        )
    for i, (beam, net) in enumerate(top(outer, carry)):
        start_state[pl.ds(2 * i * gs, gs), :] = beam
        start_state[pl.ds((2 * i + 1) * gs, gs), :] = net

    for k in range(chunks):
        for here, make in northward + southward + detour_n + detour_s:

            @pl.when(here)
            def _():
                make(k).wait_send()

        for at in range(slots):

            @pl.when(first)
            def _():
                hop_s(k, at).wait_send()

            @pl.when(last)
            def _():
                hop_n(k, at).wait_send()


def on_device(tracers, courant_x, courant_y, sunlit, cosine, albedo, absorb, scatter, weight):
    count, levels, rows, lanes = tracers.shape
    gs = absorb.shape[0]
    chunks = len(PARTS)
    slots = lax.axis_size("lat") // 2 - 1
    f32 = jnp.float32
    hbm = pl.BlockSpec(memory_space=pltpu.HBM)
    vmem = pl.BlockSpec(memory_space=pltpu.VMEM)
    dma = pltpu.SemaphoreType.DMA
    flat = levels * rows
    inner_layers = pltpu.VMEM((levels, (rows - 2) * gs, lanes), f32)
    outer_layers = pltpu.VMEM((levels, 2 * gs, lanes), f32)
    operands = (
        tracers,
        tracers.reshape(count, flat, lanes),
        courant_x.reshape(flat, lanes),
        courant_y.reshape(flat, lanes),
        sunlit,
        cosine,
        albedo,
        absorb,
        scatter,
        weight,
    )
    held = pl.pallas_call(
        kernel,
        out_shape=[pltpu.VMEM((count, flat, lanes), f32), pltpu.VMEM((flat, lanes), f32)]
        + [outer_layers] * 5
        + [pltpu.VMEM((4 * gs, lanes), f32)],
        in_specs=[hbm] * 10,
        out_specs=[vmem] * 8,
        scratch_shapes=[
            pltpu.VMEM((count, flat, lanes), f32),
            pltpu.VMEM((flat, lanes), f32),
            pltpu.VMEM((flat, lanes), f32),
            pltpu.VMEM((rows, lanes), jnp.int32),
            pltpu.VMEM((rows, lanes), f32),
            pltpu.VMEM((rows, lanes), f32),
            pltpu.VMEM(absorb.shape, f32),
            pltpu.SMEM((gs,), f32),
            pltpu.SMEM((gs,), f32),
            pltpu.VMEM((count, levels, lanes), f32),
            pltpu.VMEM((count, levels, lanes), f32),
            pltpu.VMEM((count, levels, lanes), f32),
            pltpu.VMEM((slots, 2, levels, lanes), f32),
            pltpu.VMEM((count + 1, rows, lanes), f32),
            pltpu.VMEM((count, rows, lanes), f32),
            pltpu.VMEM((count, rows, lanes), f32),
            pltpu.VMEM((count + 1, rows, lanes), f32),
        ]
        + [inner_layers] * 6
        + [dma((count + 8,)), dma((chunks, 5)), dma((chunks, 5)), dma((2,)), dma((2,))]
        + [dma((chunks, slots)), dma((chunks, slots))],
        compiler_params=pltpu.CompilerParams(
            collective_id=0, has_side_effects=True, vmem_limit_bytes=36 * 2**20
        ),
        name="advect_and_heat",
    )(*[pltpu.with_memory_space_constraint(a, pltpu.HBM) for a in operands])
    moved, heating = pl.pallas_call(
        finish,
        out_shape=[pltpu.HBM((count, flat, lanes), f32), pltpu.HBM((flat, lanes), f32)],
        in_specs=[vmem] * 8,
        out_specs=[hbm] * 2,
        scratch_shapes=[outer_layers, pltpu.VMEM((flat, lanes), f32), dma((2,))],
        compiler_params=pltpu.CompilerParams(vmem_limit_bytes=8 * 2**20),
        name="finish",
    )(*[pltpu.with_memory_space_constraint(a, pltpu.VMEM) for a in held])
    return moved.reshape(tracers.shape), heating.reshape(levels, rows, lanes)


def solution(mesh):
    in_specs = (
        P(None, None, "lat", "lon"),
        P(None, "lat", "lon"),
        P(None, "lat", "lon"),
        P("lat", "lon"),
        P("lat", "lon"),
        P("lat", "lon"),
        P(),
        P(),
        P(),
    )
    out_specs = (P(None, None, "lat", "lon"), P(None, "lat", "lon"))
    return jax.shard_map(
        on_device, mesh=mesh, in_specs=in_specs, out_specs=out_specs, check_vma=False
    )
```

```python
import functools

import jax
import jax.numpy as jnp
from jax import lax
from jax.experimental import pallas as pl
from jax.experimental.pallas import tpu as pltpu
from jax.sharding import PartitionSpec as P

MESH = pl.DeviceIdType.MESH
LOG2E = 1.4426950408889634
PARTS = ((96, 32), (48, 48), (8, 40), (0, 8))
NA, NB, SA, SB, RELAY = range(5)


def rcp(value):
    return pltpu.reciprocal(value, approx=True)


def sweep(beams, keep, nn):
    kp, kq, kd, ka, ks = keep
    levels = nn.shape[0]

    def step(level, state):
        state_new = []
        for i, (dn, beam, net) in enumerate(state):
            at = pl.ds(8 * i, 8)
            dn = kp[level, at, :] * dn + kq[level, at, :] * beam
            beam = beam * kd[level, at, :]
            below = dn * ka[level, at, :] + beam * ks[level, at, :]
            nn[level, at, :] = net - below
            state_new.append((dn, beam, below))
        return tuple(state_new)

    state = tuple((jnp.zeros_like(beam), beam, net) for beam, net in beams)
    lax.fori_loop(0, levels, step, state, unroll=8)


def summed(nn, group, i):
    levels, depth, lanes = nn.shape
    flat = nn.reshape(levels * depth, lanes)
    parts = [flat[pl.ds(group * 8 * depth + 8 * i + g, 8, stride=depth), :] for g in range(8)]
    while len(parts) > 1:
        parts = [a + b for a, b in zip(parts[::2], parts[1::2], strict=True)]
    return parts[0]


def finish(tn, heat, op, oq, od, oa, os, start_state, tn_out, heat_out, nn, full, sem):
    levels = nn.shape[0]
    rows = heat.shape[0] // levels
    moved = pltpu.make_async_copy(tn, tn_out, sem.at[0])
    moved.start()
    beams = [
        (start_state[pl.ds(16 * i, 8), :], start_state[pl.ds(16 * i + 8, 8), :]) for i in range(2)
    ]
    sweep(beams, (op, oq, od, oa, os), nn)

    def total(group, carry):
        at = pl.ds(pl.multiple_of(group * 8 * rows, 8 * rows), 8 * rows)
        full[at, :] = heat[at, :]
        for i, r in enumerate((0, rows - 1)):
            full[pl.ds(group * 8 * rows + r, 8, stride=rows), :] = summed(nn, group, i)
        return carry

    lax.fori_loop(0, levels // 8, total, 0, unroll=2)
    heated = pltpu.make_async_copy(full, heat_out, sem.at[1])
    heated.start()
    moved.wait()
    heated.wait()


def kernel(
    x4, x3, cx3, cy3, sunlit_in, cosine_in, albedo_in, absorb_in, scatter_in, weight_in,
    tn, heat, op, oq, od, oa, os, start_state,
    x, cx, cy, sunlit, cosine, albedo, absorb, scatter, weight,
    rows_n, north, south, relay, pack_e, pack_w, from_e, from_w,
    cp, cq, cd, ca, cs, nn,
    load_sem, send_sem, recv_sem, lon_send, lon_recv, relay_recv, hop_send,
):
    tracers, levels = x4.shape[0], x4.shape[1]
    rows, lanes = x4.shape[2], x4.shape[3]
    chunks = len(PARTS)
    lon, lat = lax.axis_index("lon"), lax.axis_index("lat")
    n_lon, n_lat = lax.axis_size("lon"), lax.axis_size("lat")
    has_n, has_s = lat < n_lat - 1, lat > 0
    to_n, to_s = (lon, lat + 1), (lon, lat - 1)
    to_e, to_w = (lax.rem(lon + 1, n_lon), lat), (lax.rem(lon + n_lon - 1, n_lon), lat)
    first, last = lat == 0, lat == n_lat - 1
    middle = jnp.logical_and(has_n, has_s)
    even = lax.rem(lat, 2) == 0
    via_first = jnp.logical_and(middle, even)
    via_last = jnp.logical_and(middle, jnp.logical_not(even))
    slots = relay.shape[0]
    slot = lax.div(lat - 1, 2)

    def direct(k):
        return pl.ds(0, tracers - 1 - k % 2)

    def shared(k):
        return pl.ds(tracers - 1 - k % 2, 1 + k % 2)

    pairs = (
        (cx3, cx), *[(x3.at[t], x.at[t]) for t in range(tracers)],
        (cy3, cy), (sunlit_in, sunlit), (cosine_in, cosine), (albedo_in, albedo),
        (absorb_in, absorb), (scatter_in, scatter), (weight_in, weight),
    )
    loads = [pltpu.make_async_copy(a, b, load_sem.at[i]) for i, (a, b) in enumerate(pairs)]
    for c in loads:
        c.start()

    barrier = pltpu.get_barrier_semaphore()
    partners = [
        (None, to_e),
        (None, to_w),
        (has_n, to_n),
        (has_s, to_s),
        (jnp.logical_and(middle, lat > 1), (lon, 0)),
        (jnp.logical_and(middle, lat < n_lat - 2), (lon, n_lat - 1)),
    ]
    for other in range(1, n_lat - 1):
        if other > 1:
            partners.append((first, (lon, other)))
        if other < n_lat - 2:
            partners.append((last, (lon, other)))
    for here, device in partners:
        if here is None:
            pl.semaphore_signal(barrier, inc=1, device_id=device, device_id_type=MESH)
        else:

            @pl.when(here)
            def _():
                pl.semaphore_signal(barrier, inc=1, device_id=device, device_id_type=MESH)

    peers = 2
    for here, _ in partners[2:]:
        peers = peers + here.astype(jnp.int32)
    def copy(src, dst, k, kind, device):
        return pltpu.make_async_remote_copy(
            src_ref=src,
            dst_ref=dst,
            send_sem=send_sem.at[k, kind],
            recv_sem=recv_sem.at[k, kind],
            device_id=device,
            device_id_type=MESH,
        )

    def part(k):
        return pl.ds(*PARTS[k])

    def rows_to_n(k, planes, kind):
        src, dst = rows_n.at[planes, part(k)], south.at[planes, part(k)]
        return copy(src, dst, k, kind, to_n)

    def rows_to_s(k, planes, kind):
        src, dst = x4.at[planes, part(k), 0, :], north.at[planes, part(k)]
        return copy(src, dst, k, kind, to_s)

    def send_na(k):
        return rows_to_n(k, direct(k), NA)

    def send_nb(k):
        return rows_to_n(k, shared(k), NB)

    def send_n(k):
        return rows_to_n(k, pl.ds(0, tracers), NA)

    def send_sa(k):
        return rows_to_s(k, direct(k), SA)

    def send_sb(k):
        return rows_to_s(k, shared(k), SB)

    def send_s(k):
        return rows_to_s(k, pl.ds(0, tracers), SA)

    def detour_row(k, planes_of, at, to):
        return pltpu.make_async_remote_copy(
            src_ref=planes_of,
            dst_ref=relay.at[at, pl.ds(0, 1 + k % 2), part(k)],
            send_sem=send_sem.at[k, RELAY],
            recv_sem=relay_recv.at[k, at],
            device_id=(lon, to),
            device_id_type=MESH,
        )

    def send_rs(k):
        return detour_row(k, x4.at[shared(k), part(k), 0, :], slot, 0)

    def send_rn(k):
        return detour_row(k, rows_n.at[shared(k), part(k)], slot, n_lat - 1)

    def hop(k, at, dst, kind, to):
        return pltpu.make_async_remote_copy(
            src_ref=relay.at[at, pl.ds(0, 1 + k % 2), part(k)],
            dst_ref=dst.at[shared(k), part(k)],
            send_sem=hop_send.at[k, at],
            recv_sem=recv_sem.at[k, kind],
            device_id=(lon, to),
            device_id_type=MESH,
        )

    def hop_s(k, at):
        return hop(k, at, north, SB, 2 * at + 1)

    def hop_n(k, at):
        return hop(k, at, south, NB, 2 * at + 2)

    detour_s, detour_n = [(via_first, send_rs)], [(via_last, send_rn)]
    northward = [
        (jnp.logical_and(has_n, jnp.logical_not(via_last)), send_n),
        (via_last, send_na),
    ]
    southward = [
        (jnp.logical_and(has_s, jnp.logical_not(via_first)), send_s),
        (via_first, send_sa),
    ]
    whole_s, split_s = jnp.logical_and(has_s, jnp.logical_not(even)), jnp.logical_and(has_s, even)
    whole_n, split_n = jnp.logical_and(has_n, even), jnp.logical_and(has_n, jnp.logical_not(even))
    incoming = [
        (whole_s, send_n),
        (split_s, send_na),
        (split_s, send_nb),
        (whole_n, send_s),
        (split_n, send_sa),
        (split_n, send_sb),
    ]

    def pass_on(k):
        for at in range(slots):

            @pl.when(first)
            def _():
                detour_row(k, x4.at[shared(k), part(k), 0, :], at, 0).wait_recv()
                hop_s(k, at).start()

            @pl.when(last)
            def _():
                detour_row(k, rows_n.at[shared(k), part(k)], at, n_lat - 1).wait_recv()
                hop_n(k, at).start()

    def send(k, which):
        for here, make in which:

            @pl.when(here)
            def _():
                make(k).start()

    @pl.when(last)
    def _():
        north[...] = jnp.zeros_like(north)

    @pl.when(first)
    def _():
        south[...] = jnp.zeros_like(south)

    lane = lax.broadcasted_iota(jnp.int32, (rows, lanes), 1)
    sub = lax.broadcasted_iota(jnp.int32, (rows, lanes), 0)

    def tile(level):
        return pl.ds(pl.multiple_of(level * rows, rows), rows)

    def every(level, row):
        return pl.ds(level * rows + row, 8, stride=rows)

    def pack(fields, level, packed):
        shift = lax.rem(level + 1, lanes)
        at_e, at_w = lane == level, lane == shift
        packed_new = []
        for field, (west, east) in zip(fields, packed, strict=True):
            turned = pltpu.roll(field[tile(level), :], shift, 1)
            packed_new.append((jnp.where(at_w, turned, west), jnp.where(at_e, turned, east)))
        return tuple(packed_new)

    zero = jnp.zeros((rows, lanes), jnp.float32)
    loads[0].wait()
    for t in range(0, tracers, 2):
        loads[1 + t].wait()
        loads[2 + t].wait()
        fields = [x.at[t], x.at[t + 1]] + ([cx] if t == 0 else [])
        packed = lax.fori_loop(
            0,
            levels,
            functools.partial(pack, fields),
            ((zero, zero),) * len(fields),
            unroll=levels,
        )
        for u, (west, east) in enumerate(packed[:2]):
            pack_w[t + u] = west
            pack_e[t + u] = east
        if t == 0:
            pack_e[tracers] = packed[2][1]
    go_w = pltpu.make_async_remote_copy(
        src_ref=pack_w, dst_ref=from_e, send_sem=lon_send.at[0], recv_sem=lon_recv.at[0],
        device_id=to_w, device_id_type=MESH,
    )
    go_e = pltpu.make_async_remote_copy(
        src_ref=pack_e, dst_ref=from_w, send_sem=lon_send.at[1], recv_sem=lon_recv.at[1],
        device_id=to_e, device_id_type=MESH,
    )
    pl.semaphore_wait(barrier, peers)
    go_w.start()
    go_e.start()
    for k in range(chunks):
        send(k, detour_s)
    send(0, southward)
    for c in loads[1 + tracers :]:
        c.wait()

    def gather(group, carry):
        at = pl.ds(pl.multiple_of(group * 8, 8), 8)
        flow = cy[every(group * 8, rows - 1), :]
        inward = jnp.maximum(flow, 0.0)
        for t in range(tracers):
            share = inward * x[t, every(group * 8, rows - 1), :]
            rows_n[t, at, :] = jnp.where(flow < 0.0, flow, share) if t == 0 else share
        return carry

    lax.fori_loop(0, levels // 8, gather, 0, unroll=4)
    for k in range(chunks):
        send(k, detour_n)
    send(0, northward)
    for k in range(1, chunks):
        send(k, southward)
        send(k, northward)
    go_w.wait()
    go_e.wait()
    for k in range(chunks):
        pass_on(k)
    flow = from_w[tracers]
    for t in range(tracers):
        own = pltpu.roll(pack_w[t], lanes - 1, 1)
        from_w[t] = jnp.maximum(flow, 0.0) * from_w[t] + jnp.minimum(flow, 0.0) * own

    def advect(level, carry):
        to_first = lax.rem(2 * lanes - level, lanes)
        to_last = lax.rem(2 * lanes - 2 - level, lanes)
        here_x = cx[tile(level), :]
        here_y = jnp.where(sub == rows - 1, 0.0, cy[tile(level), :])
        xp, xm = jnp.maximum(here_x, 0.0), jnp.minimum(here_x, 0.0)
        yp, ym = jnp.maximum(here_y, 0.0), jnp.minimum(here_y, 0.0)
        for t in range(tracers):
            q = x[t, tile(level), :]
            ahead = jnp.where(
                lane == lanes - 1, pltpu.roll(from_e[t], to_last, 1), pltpu.roll(q, lanes - 1, 1)
            )
            flux_e = xp * q + xm * ahead
            flux_w = jnp.where(
                lane == 0, pltpu.roll(from_w[t], to_first, 1), pltpu.roll(flux_e, 1, 1)
            )
            flux_n = yp * q + ym * pltpu.roll(q, rows - 1, 0)
            flux_s = pltpu.roll(flux_n, 1, 0)
            tn[t, tile(level), :] = q - (flux_e - flux_w) - (flux_n - flux_s)
        return carry

    gs = absorb.shape[0]
    fold = -2.0 * LOG2E
    scat, wgt = zero, zero
    for g in range(gs):
        scat = jnp.where(sub == g, scatter[g], scat)
        wgt = jnp.where(sub == g, weight[g], wgt)
    coef = [jnp.broadcast_to(absorb[:, t : t + 1], (gs, lanes)) for t in range(tracers)]
    coef[0] = coef[0] + scat
    coef = [c * fold for c in coef]
    scat = scat * (0.9 * fold)

    def spread(ref, row):
        return jnp.broadcast_to(ref[row : row + 1, :], (gs, lanes))

    def up(which, keep, level, carry):
        half_inv = [0.5 / spread(cosine, r) for r in which]
        carry_new = []
        kp, kq, kd, ka, ks = keep
        for i, (r, half, (a, s)) in enumerate(zip(which, half_inv, carry, strict=True)):
            q = [
                jnp.broadcast_to(tn[t, pl.ds(level * rows + r, 1), :], (gs, lanes))
                for t in range(tracers)
            ]
            opt = coef[0] * q[0]
            for t in range(1, tracers):
                opt = opt + coef[t] * q[t]
            single = scat * q[0] * rcp(opt)
            square = (1.0 - single) * (1.0 - 0.85 * single)
            h = square * lax.rsqrt(square)
            e = jnp.exp2(h * opt)
            direct = jnp.exp2(opt * half)
            e2 = e * e
            u = 1.0 - e2
            inv = rcp(h * (1.0 + e2) + (1.0 - 0.925 * single) * u)
            back = 0.075 * single
            refl = back * (u * inv)
            trans = (e + e) * (h * inv)
            refl_dir = back * (1.0 - direct)
            trans_dir = (0.925 / 0.075) * refl_dir
            d = rcp(1.0 - refl * a)
            p = trans * d
            sd = s * direct
            at = pl.ds(i * gs, gs)
            kp[level, at, :] = p
            kq[level, at, :] = (refl * sd + trans_dir) * d
            kd[level, at, :] = direct
            ka[level, at, :] = 1.0 - a
            ks[level, at, :] = 1.0 - s
            a_new = refl + (trans * a) * p
            s_new = refl_dir + p * (sd + a * trans_dir)
            carry_new.append((a_new, s_new))
        return tuple(carry_new)

    def ground(which):
        return tuple((spread(albedo, r), spread(albedo, r)) for r in which)

    def top(which, carry):
        beams = []
        for r, (_, s) in zip(which, carry, strict=True):
            lit = spread(sunlit, r).astype(jnp.float32)
            beam = (4.0 * lit) * wgt * spread(cosine, r)
            beams.append((beam, beam * (1.0 - s)))
        return beams

    inner = tuple(range(1, rows - 1))
    lax.fori_loop(0, levels, advect, 0, unroll=4)
    carry = ground(inner)
    carry = lax.fori_loop(
        0, levels, lambda i, c: up(inner, (cp, cq, cd, ca, cs), levels - 1 - i, c), carry, unroll=4
    )
    sweep(top(inner, carry), (cp, cq, cd, ca, cs), nn)

    def total(group, carry):
        for i, r in enumerate(inner):
            heat[pl.ds(group * 8 * rows + r, 8, stride=rows), :] = summed(nn, group, i)
        return carry

    lax.fori_loop(0, levels // 8, total, 0)

    outer = (0, rows - 1)
    carry = ground(outer)

    for k, (low, count) in enumerate(PARTS):
        for here, make in incoming:

            @pl.when(here)
            def _():
                make(k).wait_recv()

        def edges(i, c):
            level = low + 8 * i
            group = pl.ds(pl.multiple_of(level, 8), 8)
            flow_n = jnp.where(last, 0.0, cy[every(level, rows - 1), :])
            flow_s = south[0, group, :]
            np_, nm = jnp.maximum(flow_n, 0.0), jnp.minimum(flow_n, 0.0)
            sm = jnp.minimum(flow_s, 0.0)
            for t in range(tracers):
                flux_n = np_ * x[t, every(level, rows - 1), :] + nm * north[t, group, :]
                share = south[t, group, :] if t else jnp.maximum(flow_s, 0.0)
                flux_s = share + sm * x[t, every(level, 0), :]
                at_n, at_s = every(level, rows - 1), every(level, 0)
                tn[t, at_n, :] = tn[t, at_n, :] - flux_n
                tn[t, at_s, :] = tn[t, at_s, :] + flux_s
            return c

        lax.fori_loop(0, count // 8, edges, 0, unroll=2)
        start = low + count - 1
        carry = lax.fori_loop(
            0, count, lambda i, c: up(outer, (op, oq, od, oa, os), start - i, c), carry, unroll=4
        )
    for i, (beam, net) in enumerate(top(outer, carry)):
        start_state[pl.ds(2 * i * gs, gs), :] = beam
        start_state[pl.ds((2 * i + 1) * gs, gs), :] = net

    for k in range(chunks):
        for here, make in northward + southward + detour_n + detour_s:

            @pl.when(here)
            def _():
                make(k).wait_send()

        for at in range(slots):

            @pl.when(first)
            def _():
                hop_s(k, at).wait_send()

            @pl.when(last)
            def _():
                hop_n(k, at).wait_send()


def on_device(tracers, courant_x, courant_y, sunlit, cosine, albedo, absorb, scatter, weight):
    count, levels, rows, lanes = tracers.shape
    gs = absorb.shape[0]
    chunks = len(PARTS)
    slots = lax.axis_size("lat") // 2 - 1
    f32 = jnp.float32
    hbm = pl.BlockSpec(memory_space=pltpu.HBM)
    vmem = pl.BlockSpec(memory_space=pltpu.VMEM)
    dma = pltpu.SemaphoreType.DMA
    flat = levels * rows
    inner_layers = pltpu.VMEM((levels, (rows - 2) * gs, lanes), f32)
    outer_layers = pltpu.VMEM((levels, 2 * gs, lanes), f32)
    operands = (
        tracers,
        tracers.reshape(count, flat, lanes),
        courant_x.reshape(flat, lanes),
        courant_y.reshape(flat, lanes),
        sunlit,
        cosine,
        albedo,
        absorb,
        scatter,
        weight,
    )
    held = pl.pallas_call(
        kernel,
        out_shape=[pltpu.VMEM((count, flat, lanes), f32), pltpu.VMEM((flat, lanes), f32)]
        + [outer_layers] * 5
        + [pltpu.VMEM((4 * gs, lanes), f32)],
        in_specs=[hbm] * 10,
        out_specs=[vmem] * 8,
        scratch_shapes=[
            pltpu.VMEM((count, flat, lanes), f32),
            pltpu.VMEM((flat, lanes), f32),
            pltpu.VMEM((flat, lanes), f32),
            pltpu.VMEM((rows, lanes), jnp.int32),
            pltpu.VMEM((rows, lanes), f32),
            pltpu.VMEM((rows, lanes), f32),
            pltpu.VMEM(absorb.shape, f32),
            pltpu.SMEM((gs,), f32),
            pltpu.SMEM((gs,), f32),
            pltpu.VMEM((count, levels, lanes), f32),
            pltpu.VMEM((count, levels, lanes), f32),
            pltpu.VMEM((count, levels, lanes), f32),
            pltpu.VMEM((slots, 2, levels, lanes), f32),
            pltpu.VMEM((count + 1, rows, lanes), f32),
            pltpu.VMEM((count, rows, lanes), f32),
            pltpu.VMEM((count, rows, lanes), f32),
            pltpu.VMEM((count + 1, rows, lanes), f32),
        ]
        + [inner_layers] * 6
        + [dma((count + 8,)), dma((chunks, 5)), dma((chunks, 5)), dma((2,)), dma((2,))]
        + [dma((chunks, slots)), dma((chunks, slots))],
        compiler_params=pltpu.CompilerParams(
            collective_id=0, has_side_effects=True, vmem_limit_bytes=36 * 2**20
        ),
        name="advect_and_heat",
    )(*[pltpu.with_memory_space_constraint(a, pltpu.HBM) for a in operands])
    moved, heating = pl.pallas_call(
        finish,
        out_shape=[pltpu.HBM((count, flat, lanes), f32), pltpu.HBM((flat, lanes), f32)],
        in_specs=[vmem] * 8,
        out_specs=[hbm] * 2,
        scratch_shapes=[outer_layers, pltpu.VMEM((flat, lanes), f32), dma((2,))],
        compiler_params=pltpu.CompilerParams(vmem_limit_bytes=8 * 2**20),
        name="finish",
    )(*[pltpu.with_memory_space_constraint(a, pltpu.VMEM) for a in held])
    return moved.reshape(tracers.shape), heating.reshape(levels, rows, lanes)


def solution(mesh):
    in_specs = (
        P(None, None, "lat", "lon"),
        P(None, "lat", "lon"),
        P(None, "lat", "lon"),
        P("lat", "lon"),
        P("lat", "lon"),
        P("lat", "lon"),
        P(),
        P(),
        P(),
    )
    out_specs = (P(None, None, "lat", "lon"), P(None, "lat", "lon"))
    return jax.shard_map(
        on_device, mesh=mesh, in_specs=in_specs, out_specs=out_specs, check_vma=False
    )
```

```python
import functools

import jax
import jax.numpy as jnp
from jax import lax
from jax.experimental import pallas as pl
from jax.experimental.pallas import tpu as pltpu
from jax.sharding import PartitionSpec as P

MESH = pl.DeviceIdType.MESH
LOG2E = 1.4426950408889634
PARTS = ((72, 56), (8, 64), (0, 8))
NA, NB, SA, SB, RELAY = range(5)


def rcp(value):
    return pltpu.reciprocal(value, approx=True)


def sweep(beams, keep, nn):
    kp, kq, kd, ka, ks = keep
    levels = nn.shape[0]

    def step(level, state):
        state_new = []
        for i, (dn, beam, net) in enumerate(state):
            at = pl.ds(8 * i, 8)
            dn = kp[level, at, :] * dn + kq[level, at, :] * beam
            beam = beam * kd[level, at, :]
            below = dn * ka[level, at, :] + beam * ks[level, at, :]
            nn[level, at, :] = net - below
            state_new.append((dn, beam, below))
        return tuple(state_new)

    state = tuple((jnp.zeros_like(beam), beam, net) for beam, net in beams)
    lax.fori_loop(0, levels, step, state, unroll=8)


def summed(nn, group, i):
    levels, depth, lanes = nn.shape
    flat = nn.reshape(levels * depth, lanes)
    parts = [flat[pl.ds(group * 8 * depth + 8 * i + g, 8, stride=depth), :] for g in range(8)]
    while len(parts) > 1:
        parts = [a + b for a, b in zip(parts[::2], parts[1::2], strict=True)]
    return parts[0]


def finish(tn, heat, op, oq, od, oa, os, start_state, tn_out, heat_out, nn, full, sem):
    levels = nn.shape[0]
    rows = heat.shape[0] // levels
    moved = pltpu.make_async_copy(tn, tn_out, sem.at[0])
    moved.start()
    beams = [
        (start_state[pl.ds(16 * i, 8), :], start_state[pl.ds(16 * i + 8, 8), :]) for i in range(2)
    ]
    sweep(beams, (op, oq, od, oa, os), nn)

    def total(group, carry):
        at = pl.ds(pl.multiple_of(group * 8 * rows, 8 * rows), 8 * rows)
        full[at, :] = heat[at, :]
        for i, r in enumerate((0, rows - 1)):
            full[pl.ds(group * 8 * rows + r, 8, stride=rows), :] = summed(nn, group, i)
        return carry

    lax.fori_loop(0, levels // 8, total, 0, unroll=2)
    heated = pltpu.make_async_copy(full, heat_out, sem.at[1])
    heated.start()
    moved.wait()
    heated.wait()


def kernel(
    x4, x3, cx3, cy3, sunlit_in, cosine_in, albedo_in, absorb_in, scatter_in, weight_in,
    tn, heat, op, oq, od, oa, os, start_state,
    x, cx, cy, sunlit, cosine, albedo, absorb, scatter, weight,
    rows_n, north, south, relay, pack_e, pack_w, from_e, from_w,
    cp, cq, cd, ca, cs, nn,
    load_sem, send_sem, recv_sem, lon_send, lon_recv, relay_recv, hop_send,
):
    tracers, levels = x4.shape[0], x4.shape[1]
    rows, lanes = x4.shape[2], x4.shape[3]
    chunks = len(PARTS)
    lon, lat = lax.axis_index("lon"), lax.axis_index("lat")
    n_lon, n_lat = lax.axis_size("lon"), lax.axis_size("lat")
    has_n, has_s = lat < n_lat - 1, lat > 0
    to_n, to_s = (lon, lat + 1), (lon, lat - 1)
    to_e, to_w = (lax.rem(lon + 1, n_lon), lat), (lax.rem(lon + n_lon - 1, n_lon), lat)
    first, last = lat == 0, lat == n_lat - 1
    middle = jnp.logical_and(has_n, has_s)
    even = lax.rem(lat, 2) == 0
    via_first = jnp.logical_and(middle, even)
    via_last = jnp.logical_and(middle, jnp.logical_not(even))
    slots = relay.shape[0]
    slot = lax.div(lat - 1, 2)

    def direct(k):
        return pl.ds(0, tracers - 1 - k % 2)

    def shared(k):
        return pl.ds(tracers - 1 - k % 2, 1 + k % 2)

    pairs = (
        (cx3, cx), *[(x3.at[t], x.at[t]) for t in range(tracers)],
        (cy3, cy), (sunlit_in, sunlit), (cosine_in, cosine), (albedo_in, albedo),
        (absorb_in, absorb), (scatter_in, scatter), (weight_in, weight),
    )
    loads = [pltpu.make_async_copy(a, b, load_sem.at[i]) for i, (a, b) in enumerate(pairs)]
    for c in loads:
        c.start()

    barrier = pltpu.get_barrier_semaphore()
    partners = [
        (None, to_e),
        (None, to_w),
        (has_n, to_n),
        (has_s, to_s),
        (jnp.logical_and(middle, lat > 1), (lon, 0)),
        (jnp.logical_and(middle, lat < n_lat - 2), (lon, n_lat - 1)),
    ]
    for other in range(1, n_lat - 1):
        if other > 1:
            partners.append((first, (lon, other)))
        if other < n_lat - 2:
            partners.append((last, (lon, other)))
    for here, device in partners:
        if here is None:
            pl.semaphore_signal(barrier, inc=1, device_id=device, device_id_type=MESH)
        else:

            @pl.when(here)
            def _():
                pl.semaphore_signal(barrier, inc=1, device_id=device, device_id_type=MESH)

    peers = 2
    for here, _ in partners[2:]:
        peers = peers + here.astype(jnp.int32)
    def copy(src, dst, k, kind, device):
        return pltpu.make_async_remote_copy(
            src_ref=src,
            dst_ref=dst,
            send_sem=send_sem.at[k, kind],
            recv_sem=recv_sem.at[k, kind],
            device_id=device,
            device_id_type=MESH,
        )

    def part(k):
        return pl.ds(*PARTS[k])

    def rows_to_n(k, planes, kind):
        src, dst = rows_n.at[planes, part(k)], south.at[planes, part(k)]
        return copy(src, dst, k, kind, to_n)

    def rows_to_s(k, planes, kind):
        src, dst = x4.at[planes, part(k), 0, :], north.at[planes, part(k)]
        return copy(src, dst, k, kind, to_s)

    def send_na(k):
        return rows_to_n(k, direct(k), NA)

    def send_nb(k):
        return rows_to_n(k, shared(k), NB)

    def send_n(k):
        return rows_to_n(k, pl.ds(0, tracers), NA)

    def send_sa(k):
        return rows_to_s(k, direct(k), SA)

    def send_sb(k):
        return rows_to_s(k, shared(k), SB)

    def send_s(k):
        return rows_to_s(k, pl.ds(0, tracers), SA)

    def detour_row(k, planes_of, at, to):
        return pltpu.make_async_remote_copy(
            src_ref=planes_of,
            dst_ref=relay.at[at, pl.ds(0, 1 + k % 2), part(k)],
            send_sem=send_sem.at[k, RELAY],
            recv_sem=relay_recv.at[k, at],
            device_id=(lon, to),
            device_id_type=MESH,
        )

    def send_rs(k):
        return detour_row(k, x4.at[shared(k), part(k), 0, :], slot, 0)

    def send_rn(k):
        return detour_row(k, rows_n.at[shared(k), part(k)], slot, n_lat - 1)

    def hop(k, at, dst, kind, to):
        return pltpu.make_async_remote_copy(
            src_ref=relay.at[at, pl.ds(0, 1 + k % 2), part(k)],
            dst_ref=dst.at[shared(k), part(k)],
            send_sem=hop_send.at[k, at],
            recv_sem=recv_sem.at[k, kind],
            device_id=(lon, to),
            device_id_type=MESH,
        )

    def hop_s(k, at):
        return hop(k, at, north, SB, 2 * at + 1)

    def hop_n(k, at):
        return hop(k, at, south, NB, 2 * at + 2)

    detour_s, detour_n = [(via_first, send_rs)], [(via_last, send_rn)]
    northward = [
        (jnp.logical_and(has_n, jnp.logical_not(via_last)), send_n),
        (via_last, send_na),
    ]
    southward = [
        (jnp.logical_and(has_s, jnp.logical_not(via_first)), send_s),
        (via_first, send_sa),
    ]
    whole_s, split_s = jnp.logical_and(has_s, jnp.logical_not(even)), jnp.logical_and(has_s, even)
    whole_n, split_n = jnp.logical_and(has_n, even), jnp.logical_and(has_n, jnp.logical_not(even))
    incoming = [
        (whole_s, send_n),
        (split_s, send_na),
        (split_s, send_nb),
        (whole_n, send_s),
        (split_n, send_sa),
        (split_n, send_sb),
    ]

    def pass_on(k):
        for at in range(slots):

            @pl.when(first)
            def _():
                detour_row(k, x4.at[shared(k), part(k), 0, :], at, 0).wait_recv()
                hop_s(k, at).start()

            @pl.when(last)
            def _():
                detour_row(k, rows_n.at[shared(k), part(k)], at, n_lat - 1).wait_recv()
                hop_n(k, at).start()

    def send(k, which):
        for here, make in which:

            @pl.when(here)
            def _():
                make(k).start()

    @pl.when(last)
    def _():
        north[...] = jnp.zeros_like(north)

    @pl.when(first)
    def _():
        south[...] = jnp.zeros_like(south)

    lane = lax.broadcasted_iota(jnp.int32, (rows, lanes), 1)
    sub = lax.broadcasted_iota(jnp.int32, (rows, lanes), 0)

    def tile(level):
        return pl.ds(pl.multiple_of(level * rows, rows), rows)

    def every(level, row):
        return pl.ds(level * rows + row, 8, stride=rows)

    def pack(fields, level, packed):
        shift = lax.rem(level + 1, lanes)
        at_e, at_w = lane == level, lane == shift
        packed_new = []
        for field, (west, east) in zip(fields, packed, strict=True):
            turned = pltpu.roll(field[tile(level), :], shift, 1)
            packed_new.append((jnp.where(at_w, turned, west), jnp.where(at_e, turned, east)))
        return tuple(packed_new)

    zero = jnp.zeros((rows, lanes), jnp.float32)
    loads[0].wait()
    for t in range(0, tracers, 2):
        loads[1 + t].wait()
        loads[2 + t].wait()
        fields = [x.at[t], x.at[t + 1]] + ([cx] if t == 0 else [])
        packed = lax.fori_loop(
            0,
            levels,
            functools.partial(pack, fields),
            ((zero, zero),) * len(fields),
            unroll=levels,
        )
        for u, (west, east) in enumerate(packed[:2]):
            pack_w[t + u] = west
            pack_e[t + u] = east
        if t == 0:
            pack_e[tracers] = packed[2][1]
    go_w = pltpu.make_async_remote_copy(
        src_ref=pack_w, dst_ref=from_e, send_sem=lon_send.at[0], recv_sem=lon_recv.at[0],
        device_id=to_w, device_id_type=MESH,
    )
    go_e = pltpu.make_async_remote_copy(
        src_ref=pack_e, dst_ref=from_w, send_sem=lon_send.at[1], recv_sem=lon_recv.at[1],
        device_id=to_e, device_id_type=MESH,
    )
    pl.semaphore_wait(barrier, peers)
    go_w.start()
    go_e.start()
    for k in range(chunks):
        send(k, detour_s)
    send(0, southward)
    for c in loads[1 + tracers :]:
        c.wait()

    def gather(group, carry):
        at = pl.ds(pl.multiple_of(group * 8, 8), 8)
        flow = cy[every(group * 8, rows - 1), :]
        inward = jnp.maximum(flow, 0.0)
        for t in range(tracers):
            share = inward * x[t, every(group * 8, rows - 1), :]
            rows_n[t, at, :] = jnp.where(flow < 0.0, flow, share) if t == 0 else share
        return carry

    lax.fori_loop(0, levels // 8, gather, 0, unroll=4)
    for k in range(chunks):
        send(k, detour_n)
    send(0, northward)
    for k in range(1, chunks):
        send(k, southward)
        send(k, northward)
    go_w.wait()
    go_e.wait()
    for k in range(chunks):
        pass_on(k)
    flow = from_w[tracers]
    for t in range(tracers):
        own = pltpu.roll(pack_w[t], lanes - 1, 1)
        from_w[t] = jnp.maximum(flow, 0.0) * from_w[t] + jnp.minimum(flow, 0.0) * own

    def advect(level, carry):
        to_first = lax.rem(2 * lanes - level, lanes)
        to_last = lax.rem(2 * lanes - 2 - level, lanes)
        here_x = cx[tile(level), :]
        here_y = jnp.where(sub == rows - 1, 0.0, cy[tile(level), :])
        xp, xm = jnp.maximum(here_x, 0.0), jnp.minimum(here_x, 0.0)
        yp, ym = jnp.maximum(here_y, 0.0), jnp.minimum(here_y, 0.0)
        for t in range(tracers):
            q = x[t, tile(level), :]
            ahead = jnp.where(
                lane == lanes - 1, pltpu.roll(from_e[t], to_last, 1), pltpu.roll(q, lanes - 1, 1)
            )
            flux_e = xp * q + xm * ahead
            flux_w = jnp.where(
                lane == 0, pltpu.roll(from_w[t], to_first, 1), pltpu.roll(flux_e, 1, 1)
            )
            flux_n = yp * q + ym * pltpu.roll(q, rows - 1, 0)
            flux_s = pltpu.roll(flux_n, 1, 0)
            tn[t, tile(level), :] = q - (flux_e - flux_w) - (flux_n - flux_s)
        return carry

    gs = absorb.shape[0]
    fold = -2.0 * LOG2E
    scat, wgt = zero, zero
    for g in range(gs):
        scat = jnp.where(sub == g, scatter[g], scat)
        wgt = jnp.where(sub == g, weight[g], wgt)
    coef = [jnp.broadcast_to(absorb[:, t : t + 1], (gs, lanes)) for t in range(tracers)]
    coef[0] = coef[0] + scat
    coef = [c * fold for c in coef]
    scat = scat * (0.9 * fold)

    def spread(ref, row):
        return jnp.broadcast_to(ref[row : row + 1, :], (gs, lanes))

    def up(which, keep, level, carry):
        half_inv = [0.5 / spread(cosine, r) for r in which]
        carry_new = []
        kp, kq, kd, ka, ks = keep
        for i, (r, half, (a, s)) in enumerate(zip(which, half_inv, carry, strict=True)):
            q = [
                jnp.broadcast_to(tn[t, pl.ds(level * rows + r, 1), :], (gs, lanes))
                for t in range(tracers)
            ]
            opt = coef[0] * q[0]
            for t in range(1, tracers):
                opt = opt + coef[t] * q[t]
            single = scat * q[0] * rcp(opt)
            square = (1.0 - single) * (1.0 - 0.85 * single)
            h = square * lax.rsqrt(square)
            e = jnp.exp2(h * opt)
            direct = jnp.exp2(opt * half)
            e2 = e * e
            u = 1.0 - e2
            inv = rcp(h * (1.0 + e2) + (1.0 - 0.925 * single) * u)
            back = 0.075 * single
            refl = back * (u * inv)
            trans = (e + e) * (h * inv)
            refl_dir = back * (1.0 - direct)
            trans_dir = (0.925 / 0.075) * refl_dir
            d = rcp(1.0 - refl * a)
            p = trans * d
            sd = s * direct
            at = pl.ds(i * gs, gs)
            kp[level, at, :] = p
            kq[level, at, :] = (refl * sd + trans_dir) * d
            kd[level, at, :] = direct
            ka[level, at, :] = 1.0 - a
            ks[level, at, :] = 1.0 - s
            a_new = refl + (trans * a) * p
            s_new = refl_dir + p * (sd + a * trans_dir)
            carry_new.append((a_new, s_new))
        return tuple(carry_new)

    def ground(which):
        return tuple((spread(albedo, r), spread(albedo, r)) for r in which)

    def top(which, carry):
        beams = []
        for r, (_, s) in zip(which, carry, strict=True):
            lit = spread(sunlit, r).astype(jnp.float32)
            beam = (4.0 * lit) * wgt * spread(cosine, r)
            beams.append((beam, beam * (1.0 - s)))
        return beams

    inner = tuple(range(1, rows - 1))
    lax.fori_loop(0, levels, advect, 0, unroll=4)
    carry = ground(inner)
    carry = lax.fori_loop(
        0, levels, lambda i, c: up(inner, (cp, cq, cd, ca, cs), levels - 1 - i, c), carry, unroll=4
    )
    sweep(top(inner, carry), (cp, cq, cd, ca, cs), nn)

    def total(group, carry):
        for i, r in enumerate(inner):
            heat[pl.ds(group * 8 * rows + r, 8, stride=rows), :] = summed(nn, group, i)
        return carry

    lax.fori_loop(0, levels // 8, total, 0)

    outer = (0, rows - 1)
    carry = ground(outer)

    for k, (low, count) in enumerate(PARTS):
        for here, make in incoming:

            @pl.when(here)
            def _():
                make(k).wait_recv()

        def edges(i, c):
            level = low + 8 * i
            group = pl.ds(pl.multiple_of(level, 8), 8)
            flow_n = jnp.where(last, 0.0, cy[every(level, rows - 1), :])
            flow_s = south[0, group, :]
            np_, nm = jnp.maximum(flow_n, 0.0), jnp.minimum(flow_n, 0.0)
            sm = jnp.minimum(flow_s, 0.0)
            for t in range(tracers):
                flux_n = np_ * x[t, every(level, rows - 1), :] + nm * north[t, group, :]
                share = south[t, group, :] if t else jnp.maximum(flow_s, 0.0)
                flux_s = share + sm * x[t, every(level, 0), :]
                at_n, at_s = every(level, rows - 1), every(level, 0)
                tn[t, at_n, :] = tn[t, at_n, :] - flux_n
                tn[t, at_s, :] = tn[t, at_s, :] + flux_s
            return c

        lax.fori_loop(0, count // 8, edges, 0, unroll=2)
        start = low + count - 1
        carry = lax.fori_loop(
            0, count, lambda i, c: up(outer, (op, oq, od, oa, os), start - i, c), carry, unroll=4
        )
    for i, (beam, net) in enumerate(top(outer, carry)):
        start_state[pl.ds(2 * i * gs, gs), :] = beam
        start_state[pl.ds((2 * i + 1) * gs, gs), :] = net

    for k in range(chunks):
        for here, make in northward + southward + detour_n + detour_s:

            @pl.when(here)
            def _():
                make(k).wait_send()

        for at in range(slots):

            @pl.when(first)
            def _():
                hop_s(k, at).wait_send()

            @pl.when(last)
            def _():
                hop_n(k, at).wait_send()


def on_device(tracers, courant_x, courant_y, sunlit, cosine, albedo, absorb, scatter, weight):
    count, levels, rows, lanes = tracers.shape
    gs = absorb.shape[0]
    chunks = len(PARTS)
    slots = lax.axis_size("lat") // 2 - 1
    f32 = jnp.float32
    hbm = pl.BlockSpec(memory_space=pltpu.HBM)
    vmem = pl.BlockSpec(memory_space=pltpu.VMEM)
    dma = pltpu.SemaphoreType.DMA
    flat = levels * rows
    inner_layers = pltpu.VMEM((levels, (rows - 2) * gs, lanes), f32)
    outer_layers = pltpu.VMEM((levels, 2 * gs, lanes), f32)
    operands = (
        tracers,
        tracers.reshape(count, flat, lanes),
        courant_x.reshape(flat, lanes),
        courant_y.reshape(flat, lanes),
        sunlit,
        cosine,
        albedo,
        absorb,
        scatter,
        weight,
    )
    held = pl.pallas_call(
        kernel,
        out_shape=[pltpu.VMEM((count, flat, lanes), f32), pltpu.VMEM((flat, lanes), f32)]
        + [outer_layers] * 5
        + [pltpu.VMEM((4 * gs, lanes), f32)],
        in_specs=[hbm] * 10,
        out_specs=[vmem] * 8,
        scratch_shapes=[
            pltpu.VMEM((count, flat, lanes), f32),
            pltpu.VMEM((flat, lanes), f32),
            pltpu.VMEM((flat, lanes), f32),
            pltpu.VMEM((rows, lanes), jnp.int32),
            pltpu.VMEM((rows, lanes), f32),
            pltpu.VMEM((rows, lanes), f32),
            pltpu.VMEM(absorb.shape, f32),
            pltpu.SMEM((gs,), f32),
            pltpu.SMEM((gs,), f32),
            pltpu.VMEM((count, levels, lanes), f32),
            pltpu.VMEM((count, levels, lanes), f32),
            pltpu.VMEM((count, levels, lanes), f32),
            pltpu.VMEM((slots, 2, levels, lanes), f32),
            pltpu.VMEM((count + 1, rows, lanes), f32),
            pltpu.VMEM((count, rows, lanes), f32),
            pltpu.VMEM((count, rows, lanes), f32),
            pltpu.VMEM((count + 1, rows, lanes), f32),
        ]
        + [inner_layers] * 6
        + [dma((count + 8,)), dma((chunks, 5)), dma((chunks, 5)), dma((2,)), dma((2,))]
        + [dma((chunks, slots)), dma((chunks, slots))],
        compiler_params=pltpu.CompilerParams(
            collective_id=0, has_side_effects=True, vmem_limit_bytes=36 * 2**20
        ),
        name="advect_and_heat",
    )(*[pltpu.with_memory_space_constraint(a, pltpu.HBM) for a in operands])
    moved, heating = pl.pallas_call(
        finish,
        out_shape=[pltpu.HBM((count, flat, lanes), f32), pltpu.HBM((flat, lanes), f32)],
        in_specs=[vmem] * 8,
        out_specs=[hbm] * 2,
        scratch_shapes=[outer_layers, pltpu.VMEM((flat, lanes), f32), dma((2,))],
        compiler_params=pltpu.CompilerParams(vmem_limit_bytes=8 * 2**20),
        name="finish",
    )(*[pltpu.with_memory_space_constraint(a, pltpu.VMEM) for a in held])
    return moved.reshape(tracers.shape), heating.reshape(levels, rows, lanes)


def solution(mesh):
    in_specs = (
        P(None, None, "lat", "lon"),
        P(None, "lat", "lon"),
        P(None, "lat", "lon"),
        P("lat", "lon"),
        P("lat", "lon"),
        P("lat", "lon"),
        P(),
        P(),
        P(),
    )
    out_specs = (P(None, None, "lat", "lon"), P(None, "lat", "lon"))
    return jax.shard_map(
        on_device, mesh=mesh, in_specs=in_specs, out_specs=out_specs, check_vma=False
    )
```
